32 devices in a mesh: ctx: 16 (over z, y, core), wt: 2 (over x).
Axes of the slice: x: 2, y: 2, z: 4, core: 2. Of those that a mesh axis runs over, the one named last changes fastest.
Arguments:
- tokens: bfloat16 [2, 2048, 1024], P('wt', 'ctx'), may hold values from -6 to 6
- cotangent: bfloat16 [2, 2048, 1024], P('wt', 'ctx'), may hold values from -6 to 6
- pair_order: int32 [16], replicated, may hold values from 0 to 15, each once
- norm_gains: float32 [2, 1024], replicated, may hold values from 0.5 to 1.5
- head_gains: float32 [2, 128], replicated, may hold values from 1 to 1.7
- gate_head: bfloat16 [16, 1024], replicated, may hold values from -0.1875 to 0.1875
- w_query: bfloat16 [2048, 1024], P('wt'), may hold values from -0.1875 to 0.1875
- w_keyval: bfloat16 [2, 1024, 1024], P(None, 'wt'), may hold values from -0.1875 to 0.1875
- w_outproj: bfloat16 [2048, 1024], P('wt'), may hold values from -2 to 2
- w_gateup: bfloat16 [2, 3072, 1024], P(None, 'wt'), may hold values from -0.1875 to 0.1875
- w_down: bfloat16 [3072, 1024], P('wt'), may hold values from -0.109375 to 0.109375
- mom_norm: float32 [2, 1024], replicated
- mom_head: float32 [2, 128], replicated
- mom_gate_head: float32 [16, 1024], replicated
- mom_query: float32 [2048, 1024], P(('ctx', 'wt'))
- mom_keyval: float32 [2, 1024, 1024], P(None, ('ctx', 'wt'))
- mom_outproj: float32 [2048, 1024], P(('ctx', 'wt'))
- mom_gateup: float32 [2, 3072, 1024], P(None, ('ctx', 'wt'))
- mom_down: float32 [3072, 1024], P(('ctx', 'wt'))
Outputs:
- output: bfloat16 [2, 2048, 1024], P('wt', 'ctx')
- grad_input: float32 [2, 2048, 1024], P('wt', 'ctx')
- grad_norm_gains: float32 [2, 1024], replicated
- grad_head_gains: float32 [2, 128], replicated
- grad_gate_head: float32 [16, 1024], replicated
- grad_query: float32 [2048, 1024], P(('ctx', 'wt'))
- grad_keyval: float32 [2, 1024, 1024], P(None, ('ctx', 'wt'))
- grad_outproj: float32 [2048, 1024], P(('ctx', 'wt'))
- grad_gateup: float32 [2, 3072, 1024], P(None, ('ctx', 'wt'))
- grad_down: float32 [3072, 1024], P(('ctx', 'wt'))
- new_mom_norm: float32 [2, 1024], replicated
- new_mom_head: float32 [2, 128], replicated
- new_mom_gate_head: float32 [16, 1024], replicated
- new_mom_query: float32 [2048, 1024], P(('ctx', 'wt'))
- new_mom_keyval: float32 [2, 1024, 1024], P(None, ('ctx', 'wt'))
- new_mom_outproj: float32 [2048, 1024], P(('ctx', 'wt'))
- new_mom_gateup: float32 [2, 3072, 1024], P(None, ('ctx', 'wt'))
- new_mom_down: float32 [3072, 1024], P(('ctx', 'wt'))
- new_norm_gains: float32 [2, 1024], replicated
- new_head_gains: float32 [2, 128], replicated
- new_gate_head: float32 [16, 1024], replicated
- new_query: float32 [2048, 1024], P(('ctx', 'wt'))
- new_keyval: float32 [2, 1024, 1024], P(None, ('ctx', 'wt'))
- new_outproj: float32 [2048, 1024], P(('ctx', 'wt'))
- new_gateup: float32 [2, 3072, 1024], P(None, ('ctx', 'wt'))
- new_down: float32 [3072, 1024], P(('ctx', 'wt'))
The draws below stay inside these ranges and needn't reach their ends.
Inputs may be any that keep to these rules, and one draw needn't show every extreme that they name: The rows of stored block i of 128 rows hold, first, the positions of block pair_order[i] of 64 positions and then those of block 31 - pair_order[i]; each value appears once.
All inputs are finite; a program needn't handle non-finite values.
Results may differ from the reference program's by a relative error of at most 0.022.
Values may be sent and summed in bfloat16 or wider, within the bound.
No kernel may reach another device: no remote copies, remote signals or barrier semaphores. Data moves between devices by JAX's collectives and lax.ppermute only.
A program may use at most 384 MiB of HBM per device.

```python
import math
import jax
import jax.numpy as jnp
from jax import lax

D = 1024
HEADS = 16
KV_HEADS = 8
HEAD_DIM = 128
FF = 3072
NS_STEPS = 5
SEQ = 2048
SEQS = 2
PAIRS = 16


def moment_like(key, shape, spread):
    return spread * jnp.clip(jax.random.normal(key, shape, jnp.float32), -6.0, 6.0)


def base_spread():
    return 0.1 * jnp.sqrt(jnp.float32(SEQ * SEQS))


def draw_mom_norm(key, part):
    return moment_like(jax.random.fold_in(key, 11), (2, D), base_spread())


def draw_mom_head(key, part):
    return moment_like(jax.random.fold_in(key, 12), (2, HEAD_DIM), base_spread())


def draw_mom_gate_head(key, part):
    return moment_like(jax.random.fold_in(key, 13), (HEADS, D), 50.0 * base_spread())


def draw_mom_query(key, part):
    return moment_like(jax.random.fold_in(key, 14), (HEADS * HEAD_DIM, D), base_spread())


def draw_mom_keyval(key, part):
    return moment_like(jax.random.fold_in(key, 15), (2, KV_HEADS * HEAD_DIM, D), base_spread())


def draw_mom_outproj(key, part):
    return moment_like(jax.random.fold_in(key, 16), (HEADS * HEAD_DIM, D), base_spread())


def draw_mom_gateup(key, part):
    return moment_like(jax.random.fold_in(key, 17), (2, FF, D), base_spread())


def draw_mom_down(key, part):
    return moment_like(jax.random.fold_in(key, 18), (FF, D), base_spread())


def block_levels(stream_key, shape, split, low, high):
    gain = 1.0
    for dim, parts in split:
        draws = jax.random.uniform(jax.random.fold_in(jax.random.fold_in(stream_key, 6), dim), (parts,), jnp.float32, low / len(split), high / len(split))
        gain = gain * jnp.repeat(jnp.exp(draws), shape[dim] // parts).reshape((-1,) + (1,) * (len(shape) - 1 - dim))
    return gain


def gaussian(own_key, dims, width, reach, cuts=(), kind=jnp.bfloat16):
    level = block_levels(own_key, dims, cuts, -0.22, 0.18) if cuts else 1.0
    entries = jax.random.normal(own_key, dims, jnp.float32) * width * level
    return jnp.minimum(jnp.maximum(entries, -reach), reach).astype(kind)


def setup_inputs(seed: int = 0) -> dict:
    seeds = jax.random.split(jax.random.key(seed), 20)
    return {
        "tokens": gaussian(seeds[0], (SEQS, SEQ, D), 1.0, 6.0, ((0, 2), (1, 16))),
        "cotangent": gaussian(seeds[1], (SEQS, SEQ, D), 1.0, 6.0, ((0, 2), (1, 16))),
        "pair_order": jax.random.permutation(seeds[2], PAIRS).astype(jnp.int32),
        "norm_gains": jnp.clip(1.0 + 0.1 * jax.random.normal(seeds[3], (2, D), jnp.float32), 0.5, 1.5),
        "head_gains": jnp.clip(jax.random.uniform(seeds[4], (2, HEAD_DIM), jnp.float32, 1.0, 1.7), 1.0, 1.7),
        "gate_head": gaussian(seeds[5], (HEADS, D), D ** -0.5, 0.1875),
        "w_query": gaussian(seeds[6], (HEADS * HEAD_DIM, D), D ** -0.5, 0.1875, ((0, 2),)),
        "w_keyval": gaussian(seeds[7], (2, KV_HEADS * HEAD_DIM, D), D ** -0.5, 0.1875, ((1, 2),)),
        "w_outproj": gaussian(seeds[8], (HEADS * HEAD_DIM, D), (max(1, 16384 // SEQ)) ** -0.5, 2.0, ((0, 2),)),
        "w_gateup": gaussian(seeds[9], (2, FF, D), D ** -0.5, 0.1875, ((1, 2),)),
        "w_down": gaussian(seeds[10], (FF, D), FF ** -0.5, 0.109375, ((0, 2),)),
        "mom_norm": draw_mom_norm(jax.random.fold_in(seeds[19], 71), 0),
        "mom_head": draw_mom_head(jax.random.fold_in(seeds[19], 71), 0),
        "mom_gate_head": draw_mom_gate_head(jax.random.fold_in(seeds[19], 71), 0),
        "mom_query": draw_mom_query(jax.random.fold_in(seeds[19], 71), 0),
        "mom_keyval": draw_mom_keyval(jax.random.fold_in(seeds[19], 71), 0),
        "mom_outproj": draw_mom_outproj(jax.random.fold_in(seeds[19], 71), 0),
        "mom_gateup": draw_mom_gateup(jax.random.fold_in(seeds[19], 71), 0),
        "mom_down": draw_mom_down(jax.random.fold_in(seeds[19], 71), 0),
    }


HIGH_PRECISION = lax.Precision.HIGHEST
NORM_EPS = 1e-06
ROPE_BASE = 1000000.0
SCHULZ_FIRST = 3.4445
SCHULZ_SECOND = -4.775
SCHULZ_THIRD = 2.0315
MOMENT_DECAY = 0.5
MATRIX_RATE = 0.03
VECTOR_RATE = 0.003

@jax.custom_vjp
def low(v):
    return lax.optimization_barrier(v.astype(jnp.bfloat16)).astype(jnp.float32)

@jax.custom_vjp
def low_back(v):
    return v

def low_keep(v):
    return (low(v), None)

def low_pass(kept, grad):
    return (grad,)

def back_keep(v):
    return (v, None)

def back_low(kept, grad):
    return (low(grad),)
low.defvjp(low_keep, low_pass)
low_back.defvjp(back_keep, back_low)

def positions(first_row, rows_in, pair_order, tok_dev):
    row_ids = first_row + jnp.arange(rows_in, dtype=jnp.int32)
    device_ids = row_ids // tok_dev
    offsets = row_ids % tok_dev
    piece_len = tok_dev // 2
    cycle_ids = jnp.arange(pair_order.shape[0], dtype=jnp.int32)
    owned = lax.optimization_barrier(jnp.sum(jnp.where(device_ids[:, None] == cycle_ids[None, :], pair_order[None, :], 0), axis=1)).astype(jnp.int32)
    block_ids = jnp.where(offsets < piece_len, owned, 2 * pair_order.shape[0] - 1 - owned)
    return (block_ids * piece_len + offsets % piece_len).astype(jnp.int32)

def rope_tables(token_place, head_dim):
    half_dim = head_dim // 2
    inverse = ROPE_BASE ** (-(2.0 * jnp.arange(half_dim, dtype=jnp.float32)) / head_dim)
    angles = token_place.astype(jnp.float32)[:, None] * inverse[None, :]
    return (jnp.cos(angles)[:, None, :], jnp.sin(angles)[:, None, :])

def rotate(values_in, cosine, sine_part):
    half_dim = values_in.shape[-1] // 2
    leading = values_in[..., :half_dim]
    trailing = values_in[..., half_dim:]
    return jnp.concatenate([leading * cosine - trailing * sine_part, trailing * cosine + leading * sine_part], axis=-1)

def rms_scale(values_in):
    return lax.rsqrt(lax.optimization_barrier(jnp.mean(values_in * values_in, axis=-1, keepdims=True)) + NORM_EPS)

def attend(query_rows, key_rows, value_rows, token_place):
    seq_len, head_count, head_dim = query_rows.shape
    kv_count = key_rows.shape[1]
    group_len = head_count // kv_count
    block_len = math.gcd(512, seq_len)
    scale_factor = 1.0 / math.sqrt(head_dim)
    grouped = query_rows.reshape(seq_len // block_len, block_len, kv_count, group_len, head_dim)
    spots = token_place.reshape(seq_len // block_len, block_len)

    def one_block(pieces):
        rows_here, spot_here = pieces
        raw_scores = jnp.einsum('qkgd,nkd->kgqn', rows_here, key_rows, precision=HIGH_PRECISION)
        allowed = token_place[None, None, None, :] <= spot_here[None, None, :, None]
        weights = jnp.where(allowed, jnp.exp(low_back(raw_scores) * scale_factor), 0.0)
        weight_total = lax.optimization_barrier(jnp.sum(weights, axis=-1))
        weighted_sum = low_back(jnp.einsum('kgqn,nkd->qkgd', low(weights), value_rows, precision=HIGH_PRECISION))
        return weighted_sum / jnp.transpose(weight_total, (2, 0, 1))[..., None]
    result = lax.map(jax.checkpoint(one_block), (grouped, spots))
    return result.reshape(seq_len, head_count, head_dim)

def sequence_forward(inputs, pair_order, params):
    norm_gains, head_gains, gate_head, w_query, w_keyval, w_outproj, w_gateup, w_down = params
    seq_len = inputs.shape[0]
    tok_dev = seq_len // pair_order.shape[0]
    head_count = gate_head.shape[0]
    head_dim = head_gains.shape[1]
    kv_count = w_keyval.shape[1] // head_dim
    token_place = positions(0, seq_len, pair_order, tok_dev)
    cosine, sine_part = rope_tables(token_place, head_dim)
    normed = low(inputs * rms_scale(inputs) * norm_gains[0])
    query_raw = low_back(jnp.dot(normed, w_query.T, precision=HIGH_PRECISION)).reshape(seq_len, head_count, head_dim)
    query_rows = low(rotate(query_raw * rms_scale(query_raw) * head_gains[0], cosine, sine_part))
    key_raw = low_back(jnp.dot(normed, w_keyval[0].T, precision=HIGH_PRECISION)).reshape(seq_len, kv_count, head_dim)
    key_rows = low(rotate(key_raw * rms_scale(key_raw) * head_gains[1], cosine, sine_part))
    value_rows = low(low_back(jnp.dot(normed, w_keyval[1].T, precision=HIGH_PRECISION))).reshape(seq_len, kv_count, head_dim)
    gate_logit = low_back(jnp.dot(normed, gate_head.T, precision=HIGH_PRECISION))
    attended = attend(query_rows, key_rows, value_rows, token_place)
    gated_rows = low((attended * jax.nn.sigmoid(gate_logit)[:, :, None]).reshape(seq_len, head_count * head_dim))
    middle = inputs + low_back(jnp.dot(gated_rows, w_outproj, precision=HIGH_PRECISION))
    hidden_in = low(middle * rms_scale(middle) * norm_gains[1])
    gate_part = low_back(jnp.dot(hidden_in, w_gateup[0].T, precision=HIGH_PRECISION))
    up_part = low_back(jnp.dot(hidden_in, w_gateup[1].T, precision=HIGH_PRECISION))
    hidden = low(jax.nn.silu(gate_part) * up_part)
    return middle + low_back(jnp.dot(hidden, w_down, precision=HIGH_PRECISION))

def orthogonal(moment):
    current = moment / (jnp.sqrt(jnp.sum(moment * moment)) + 1e-07)
    for sweep in range(NS_STEPS):
        gram = jnp.dot(current.T, current, precision=HIGH_PRECISION)
        product = jnp.dot(current, gram, precision=HIGH_PRECISION)
        current = SCHULZ_FIRST * current + SCHULZ_SECOND * product + SCHULZ_THIRD * jnp.dot(product, gram, precision=HIGH_PRECISION)
    return current

def matrix_step(weight, moment, gradient, boost=1.0):
    new_moment = MOMENT_DECAY * moment + (1.0 - MOMENT_DECAY) * gradient
    new_weight = weight - boost * MATRIX_RATE * math.sqrt(weight.shape[0]) * orthogonal(new_moment)
    return (new_moment, new_weight)

def reference(tokens, cotangent, pair_order, norm_gains, head_gains, gate_head, w_query, w_keyval, w_outproj, w_gateup, w_down, mom_norm, mom_head, mom_gate_head, mom_query, mom_keyval, mom_outproj, mom_gateup, mom_down):
    params = (norm_gains.astype(jnp.float32), head_gains.astype(jnp.float32), gate_head.astype(jnp.float32), w_query.astype(jnp.float32), w_keyval.astype(jnp.float32), w_outproj.astype(jnp.float32), w_gateup.astype(jnp.float32), w_down.astype(jnp.float32))
    inputs = tokens.astype(jnp.float32)

    def whole(all_inputs, all_params):
        return lax.map(lambda one_seq: sequence_forward(one_seq, pair_order, all_params), all_inputs)
    result, pullback = jax.vjp(whole, inputs, params)
    grad_input, grads = pullback(cotangent.astype(jnp.float32))
    g_norm, g_head, g_gate, g_query, g_keyval, g_outproj, g_gateup, g_down = grads
    new_mom_norm = MOMENT_DECAY * mom_norm + (1.0 - MOMENT_DECAY) * g_norm
    new_mom_head = MOMENT_DECAY * mom_head + (1.0 - MOMENT_DECAY) * g_head
    new_mom_gate = MOMENT_DECAY * mom_gate_head + (1.0 - MOMENT_DECAY) * g_gate
    new_norm = params[0] - VECTOR_RATE * new_mom_norm
    new_head = params[1] - VECTOR_RATE * new_mom_head
    new_gate = params[2] - VECTOR_RATE * new_mom_gate
    out_boost = math.sqrt(D / max(1, 16384 // SEQ))
    mq, wq_new = matrix_step(params[3], mom_query, g_query)
    mk, wk_new = matrix_step(params[4][0], mom_keyval[0], g_keyval[0])
    mv, wv_new = matrix_step(params[4][1], mom_keyval[1], g_keyval[1])
    mo, wo_new = matrix_step(params[5], mom_outproj, g_outproj, out_boost)
    mg, wg_new = matrix_step(params[6][0], mom_gateup[0], g_gateup[0])
    mu, wu_new = matrix_step(params[6][1], mom_gateup[1], g_gateup[1])
    md, wd_new = matrix_step(params[7], mom_down, g_down)
    return (result.astype(jnp.bfloat16), grad_input, g_norm, g_head, g_gate, g_query, g_keyval, g_outproj, g_gateup, g_down, new_mom_norm, new_mom_head, new_mom_gate, mq, jnp.stack([mk, mv]), mo, jnp.stack([mg, mu]), md, new_norm, new_head, new_gate, wq_new, jnp.stack([wk_new, wv_new]), wo_new, jnp.stack([wg_new, wu_new]), wd_new)
```

```python
import functools
import math

import jax
import jax.numpy as jnp
from jax import lax
from jax.experimental import pallas as pl
from jax.experimental.pallas import tpu as pltpu
from jax.sharding import Mesh, PartitionSpec as P

NS_STEPS = 5
NORM_EPS = 1e-06
ROPE_BASE = 1000000.0
NS_A = 3.4445
NS_B = -4.775
NS_C = 2.0315
MATRIX_RATE = 0.03
VECTOR_RATE = 0.003
CTX = ("h", "m", "i", "b", "c")
ALL = CTX + ("x",)
F32 = jnp.float32
BF16 = jnp.bfloat16


def nt(p, q):
    return lax.dot_general(p, q, (((1,), (1,)), ((), ())), preferred_element_type=F32)


def nn(p, q):
    return lax.dot_general(p, q, (((1,), (0,)), ((), ())), preferred_element_type=F32)


def tn(p, q):
    return lax.dot_general(p, q, (((0,), (0,)), ((), ())), preferred_element_type=F32)


def flip(v, *axes):
    last = 2 ** len(axes) - 1
    return lax.ppermute(v, tuple(sorted(axes, key=ALL.index)), [(j, j ^ last) for j in range(last + 1)])


NEAR = (("x",), ("b",), ("b", "x"))


def gather_near(v):
    return [v] + [flip(v, *axes) for axes in NEAR]


def pieces_far(near):
    return near + [flip(member, "c") for member in near]


def join_kernel(*refs):
    ins, out, sems = refs[:-2], refs[-2], refs[-1]
    rows = ins[0].shape[0]
    run_copies([(ref, out.at[pl.ds(k * rows, rows)]) for k, ref in enumerate(ins)], sems)


def join(pieces):
    rows, width = pieces[0].shape
    count = len(pieces)
    return pl.pallas_call(
        join_kernel,
        out_shape=jax.ShapeDtypeStruct((count * rows, width), pieces[0].dtype),
        in_specs=[HBM_SPEC] * count,
        out_specs=VMEM_SPEC,
        scratch_shapes=[pltpu.SemaphoreType.DMA((count,))],
        compiler_params=SMALL,
        cost_estimate=pl.CostEstimate(
            flops=0, bytes_accessed=4 * count * rows * width, transcendentals=0
        ),
        name="join",
    )(*pieces)


def gather_far(near):
    return join(pieces_far(near))


def gather_group(v):
    return gather_far(gather_near(v))


def sum_core(part):
    half = part.shape[0] // 2
    return part[:half] + flip(part[half:].astype(BF16), "c").astype(F32)


def sum_near(part):
    rows = part.shape[0] // 4
    low = part.astype(BF16)
    total = part[:rows]
    for slot, axes in enumerate(NEAR, 1):
        total = total + flip(low[slot * rows : (slot + 1) * rows], *axes).astype(F32)
    return total


def sum_group(part):
    return sum_near(sum_core(part))


def sum_flips(v, flips):
    return sum((flip(v, *axes) for axes in flips), v)


def swap_halves(v, my_half, my_x):
    other = lax.ppermute(v, ("h", "x"), [(1, 2), (2, 1)])
    return jnp.where(my_half == my_x, v, other)


DOWN, NONE, GATE, UP = range(4)
QUERY, OUT, KEY, VALUE = range(4)

def trade(v, axes):
    return lax.all_to_all(v, axes, split_axis=0, concat_axis=0, tiled=True)


def turned(v):
    return jnp.stack([v[0], v[2], v[1], v[3]])


def fold_pairs(q):
    return [(i * 2 + b, b * q + i) for i in range(q) for b in range(2)]


def to_home(items, q, token):
    if q > 1:
        items = lax.ppermute(items, ("i", "b"), [(d, s) for s, d in fold_pairs(q)])
    return trade(turned(tie(trade(items, ("h", "m")), token)), ("c", "x"))


def to_owner(blocks, q, token):
    items = trade(tie(turned(trade(blocks, ("c", "x"))), token), ("h", "m"))
    if q > 1:
        items = lax.ppermute(items, ("i", "b"), fold_pairs(q))
    return items


VMEM_SPEC = pl.BlockSpec(memory_space=pltpu.VMEM)
SMEM_SPEC = pl.BlockSpec(memory_space=pltpu.SMEM)
SMALL = pltpu.CompilerParams(vmem_limit_bytes=32 * 2**20)
LARGE = pltpu.CompilerParams(vmem_limit_bytes=60 * 2**20)


HBM_SPEC = pl.BlockSpec(memory_space=pl.ANY)
FAR_SPEC = pl.BlockSpec(memory_space=pltpu.HBM)


def run_copies(pairs, sems):
    copies = [pltpu.make_async_copy(p, q, sems.at[k]) for k, (p, q) in enumerate(pairs)]
    for copy in copies:
        copy.start()
    for copy in copies:
        copy.wait()


def slices_kernel(sub_ref, wq, wkv, wo, wgu, wd, gate, w_in, o_out, gu_out, d_out, sems):
    sub = sub_ref[0, 0]
    q_rows, kv_rows = o_out.shape[0], wkv.shape[1] // 4

    def part(ref, rows):
        return ref.at[pl.ds(pl.multiple_of(sub * rows, rows), rows)]

    pairs = [
        (part(wq, q_rows), w_in.at[pl.ds(0, q_rows)]),
        (part(wkv.at[0], kv_rows), w_in.at[pl.ds(q_rows, kv_rows)]),
        (part(wkv.at[1], kv_rows), w_in.at[pl.ds(q_rows + kv_rows, kv_rows)]),
        (gate, w_in.at[pl.ds(q_rows + 2 * kv_rows, gate.shape[0])]),
        (part(wo, q_rows), o_out),
    ]
    pairs += [(part(wgu.at[g], d_out.shape[0]), gu_out.at[g]) for g in range(2)]
    pairs.append((part(wd, d_out.shape[0]), d_out))
    run_copies(pairs, sems)


def weight_slices(sub, w_query, w_keyval, w_outproj, w_gateup, w_down, gate):
    width = w_query.shape[1]
    q_rows, kv_rows = w_query.shape[0] // 4, w_keyval.shape[1] // 4
    ff_rows = w_down.shape[0] // 4
    w_in, wo, wgu, wd = pl.pallas_call(
        slices_kernel,
        out_shape=[
            jax.ShapeDtypeStruct((q_rows + 2 * kv_rows + gate.shape[0], width), BF16),
            jax.ShapeDtypeStruct((q_rows, width), BF16),
            jax.ShapeDtypeStruct((2, ff_rows, width), BF16),
            jax.ShapeDtypeStruct((ff_rows, width), BF16),
        ],
        in_specs=[SMEM_SPEC] + [FAR_SPEC] * 5 + [HBM_SPEC],
        out_specs=[VMEM_SPEC] * 4,
        scratch_shapes=[pltpu.SemaphoreType.DMA((8,))],
        compiler_params=LARGE,
        cost_estimate=pl.CostEstimate(flops=0, bytes_accessed=2**23, transcendentals=0),
        name="slices",
    )(
        sub.reshape(1, 1),
        w_query,
        w_keyval,
        w_outproj,
        w_gateup,
        w_down,
        gate,
    )
    return w_in, wo, wgu.reshape(2 * ff_rows, width), wd


def owned_kernel(spot_ref, *refs):
    ins, outs, sems = refs[:5], refs[-3:-1], refs[-1]
    pairs = []
    for k, out in enumerate(outs):
        spot, at = spot_ref[0, k], 0
        for ref in ins:
            rows = ref.shape[-2] // row_blocks(out, ins)
            span = pl.ds(pl.multiple_of(spot * rows, rows), rows)
            for part in [ref.at[j] for j in range(2)] if len(ref.shape) == 3 else [ref]:
                pairs.append((part.at[span], out.at[pl.ds(at, rows)]))
                at += rows
    run_copies(pairs, sems)


def row_blocks(out, ins):
    total = sum(ref.shape[-2] * (2 if len(ref.shape) == 3 else 1) for ref in ins)
    return total // out.shape[0]


def owned_rows(spots, weights, n, *tokens):
    rows = sum(w.shape[-2] * (2 if w.ndim == 3 else 1) for w in weights) // (4 * n)
    out = jax.ShapeDtypeStruct((rows, weights[0].shape[-1]), BF16)
    return pl.pallas_call(
        owned_kernel,
        out_shape=[out, out],
        in_specs=[SMEM_SPEC] + [FAR_SPEC] * 5 + [HBM_SPEC] * len(tokens),
        out_specs=[VMEM_SPEC] * 2,
        scratch_shapes=[pltpu.SemaphoreType.DMA((14,))],
        compiler_params=LARGE,
        cost_estimate=pl.CostEstimate(flops=0, bytes_accessed=2**22, transcendentals=0),
        name="owned",
    )(spots, *weights, *tokens)


def tie(value, *tokens):
    return pl.pallas_call(
        lambda *refs: None,
        out_shape=jax.ShapeDtypeStruct(value.shape, value.dtype),
        in_specs=[HBM_SPEC] * (1 + len(tokens)),
        out_specs=HBM_SPEC,
        input_output_aliases={0: 0},
        cost_estimate=pl.CostEstimate(flops=0, bytes_accessed=0, transcendentals=0),
        name="tie",
    )(value, *tokens)


def pack_kernel(places, ins, *refs):
    out = refs[-1]
    height, width = out.shape[1:]
    filled = set()
    for ref, item in zip(refs[:ins], places):
        rows = ref.shape[-2]
        for j, member in enumerate(item):
            source = ref[j] if len(ref.shape) == 3 else ref[...]
            out[member, :rows] = source.astype(BF16)
            if rows < height:
                out[member, rows:] = jnp.zeros((height - rows, width), BF16)
            filled.add(member)
    for member in range(4):
        if member not in filled:
            out[member] = jnp.zeros((height, width), BF16)


def pack(arrays, places, height, *tokens):
    width = arrays[0].shape[-1]
    return pl.pallas_call(
        functools.partial(pack_kernel, places, len(arrays)),
        out_shape=jax.ShapeDtypeStruct((4, height, width), BF16),
        in_specs=[VMEM_SPEC] * len(arrays) + [HBM_SPEC] * len(tokens),
        out_specs=VMEM_SPEC,
        compiler_params=SMALL,
        cost_estimate=pl.CostEstimate(flops=0, bytes_accessed=24 * height * width, transcendentals=0),
        name="pack",
    )(*arrays, *tokens)


def held_kernel(v_ref, *refs):
    refs[-1][...] = v_ref[...]


def held(v, *tokens):
    return pl.pallas_call(
        held_kernel,
        out_shape=jax.ShapeDtypeStruct(v.shape, v.dtype),
        in_specs=[VMEM_SPEC] + [HBM_SPEC] * len(tokens),
        out_specs=VMEM_SPEC,
        compiler_params=SMALL,
        cost_estimate=pl.CostEstimate(flops=0, bytes_accessed=4 * v.size, transcendentals=0),
        name="held",
    )(v, *tokens)


def settle_kernel(places, rates, items, *refs):
    if rates is None:
        count = len(places)
        olds, outs = refs[:count], refs[count:]
    else:
        old_ref, outs = refs[0], refs[1:]
    for a, item in enumerate(places):
        rows = outs[a].shape[-2]
        for j, place in enumerate(item):
            at = (j,) if len(outs[a].shape) == 3 else (slice(None),)
            member, first = place if rates is not None else (place, 0)
            value = items[member, :rows].astype(F32)
            if rates is None:
                outs[a][at] = value
                outs[count + a][at] = 0.5 * olds[a][at] + 0.5 * value
            else:
                old = old_ref[first : first + rows, :].astype(F32)
                outs[a][at] = old - rates[member] * value


def settle(items, olds, shapes, places, rates):
    shapes = [jax.ShapeDtypeStruct(v.shape, F32) for v in shapes]
    shapes = shapes * (2 if rates is None else 1)
    return pl.pallas_call(
        functools.partial(settle_kernel, places, rates),
        out_shape=shapes,
        in_specs=[VMEM_SPEC] * (1 + len(olds)),
        out_specs=[VMEM_SPEC] * len(shapes),
        compiler_params=SMALL,
        cost_estimate=pl.CostEstimate(flops=0, bytes_accessed=12 * items.size, transcendentals=0),
        name="settle",
    )(items, *olds)


TILE = 512


def tile_at(j):
    return pl.ds(pl.multiple_of(j * TILE, TILE), TILE)


def attend_kernel(scale, q_ref, k_ref, v_ref, qp_ref, kp_ref, o_ref):
    @pl.loop(0, q_ref.shape[0] // TILE)
    def _(i):
        query, place = q_ref[tile_at(i), :], qp_ref[tile_at(i), :]

        def step(j, acc):
            scores = nt(query, k_ref[tile_at(j), :])
            weights = jnp.where(kp_ref[:, tile_at(j)] <= place, jnp.exp2(scores * scale), 0.0)
            return acc + nn(weights.astype(BF16), v_ref[tile_at(j), :])

        o_ref[tile_at(i), :] = lax.fori_loop(
            0, k_ref.shape[0] // TILE, step, jnp.zeros((TILE, v_ref.shape[1]), F32)
        )


def attend(query, key, wide, q_place, k_place, scale):
    rows, dim = query.shape
    keys = key.shape[0]
    out = pl.pallas_call(
        functools.partial(attend_kernel, scale * math.log2(math.e)),
        out_shape=jax.ShapeDtypeStruct((rows, 2 * dim), F32),
        in_specs=[VMEM_SPEC] * 5,
        out_specs=VMEM_SPEC,
        compiler_params=pltpu.CompilerParams(vmem_limit_bytes=40 * 2**20),
        cost_estimate=pl.CostEstimate(
            flops=22 * rows * keys * dim, bytes_accessed=rows * dim * 12, transcendentals=0
        ),
        name="attend",
    )(query, key, wide, q_place[:, None], k_place[None, :])
    return out[:, :dim], out[:, dim : dim + 1]


def attend_back_kernel(
    scale, q_ref, w_ref, cr_ref, qp_ref, k_ref, v_ref, kp_ref, dq_ref, dk_ref, dv_ref
):
    dk_ref[...] = jnp.zeros_like(dk_ref)
    dv_ref[...] = jnp.zeros_like(dv_ref)
    grow = scale * math.log2(math.e)

    @pl.loop(0, q_ref.shape[0] // TILE)
    def _(i):
        query, back = q_ref[tile_at(i), :], w_ref[tile_at(i), :]
        place, corr = qp_ref[:, tile_at(i)], cr_ref[:, tile_at(i)]

        def step(j, acc):
            span = tile_at(j)
            key = k_ref[span, :]
            weights = jnp.where(kp_ref[span, :] <= place, jnp.exp2(nt(key, query) * grow), 0.0)
            push = nt(v_ref[span, :], back)
            dscore = (weights * (push - corr) * scale).astype(BF16)
            dv_ref[span, :] += nn(weights.astype(BF16), back)
            dk_ref[span, :] += nn(dscore, query)
            return acc + tn(dscore, key)

        dq_ref[tile_at(i), :] = lax.fori_loop(
            0, k_ref.shape[0] // TILE, step, jnp.zeros(query.shape, F32)
        )


def attend_back(query, back, corr, key, value, q_place, k_place, scale):
    rows, dim = query.shape
    keys = key.shape[0]
    return pl.pallas_call(
        functools.partial(attend_back_kernel, scale),
        out_shape=(
            jax.ShapeDtypeStruct((rows, dim), F32),
            jax.ShapeDtypeStruct((keys, dim), F32),
            jax.ShapeDtypeStruct((keys, dim), F32),
        ),
        in_specs=[VMEM_SPEC] * 7,
        out_specs=[VMEM_SPEC] * 3,
        compiler_params=pltpu.CompilerParams(vmem_limit_bytes=40 * 2**20),
        cost_estimate=pl.CostEstimate(
            flops=40 * rows * keys * dim, bytes_accessed=rows * dim * 16, transcendentals=0
        ),
        name="attend_back",
    )(query, back, corr[None, :], q_place[None, :], key, value, k_place[:, None])


def rms_scale(v):
    return lax.rsqrt(jnp.mean(v * v, axis=-1, keepdims=True) + NORM_EPS)


def rotate(v, cosine, sine):
    half = v.shape[-1] // 2
    lead, trail = v[..., :half], v[..., half:]
    return jnp.concatenate([lead * cosine - trail * sine, trail * cosine + lead * sine], axis=-1)


def rotate_back(g, cosine, sine):
    half = g.shape[-1] // 2
    lead, trail = g[..., :half], g[..., half:]
    return jnp.concatenate([lead * cosine + trail * sine, trail * cosine - lead * sine], axis=-1)


def norm_back(grad, scaled, rscale, gains):
    pushed = grad * gains
    return rscale * (pushed - scaled * jnp.mean(pushed * scaled, axis=-1, keepdims=True))


def mirror(ref, tile):
    for j in range(ref.shape[0] // tile):
        for i in range(j):
            block = ref[i * tile : (i + 1) * tile, j * tile : (j + 1) * tile].astype(F32)
            ref[j * tile : (j + 1) * tile, i * tile : (i + 1) * tile] = block.T.astype(BF16)


def schulz_kernel(count, start_ref, *refs):
    pieces = refs[:count]
    o_ref, x_ref, x_own, e_gram, e_poly, e_half, gram, poly, half, sems = refs[-10:]
    piece = pieces[0].shape[0]
    copies = [
        pltpu.make_async_copy(ref, x_ref.at[pl.ds(k * piece, piece)], sems.at[k])
        for k, ref in enumerate(pieces)
    ]
    for copy in copies:
        copy.start()
    for copy in copies:
        copy.wait()
    chunk = min(1024, x_ref.shape[0])
    width = x_ref.shape[1]
    own = o_ref.shape[0]
    tile = 256
    blocks = [(slice(0, (j + 1) * tile), slice(j * tile, (j + 1) * tile)) for j in range(width // tile)]
    diag = (
        lax.broadcasted_iota(jnp.int32, (tile, tile), 0)
        == lax.broadcasted_iota(jnp.int32, (tile, tile), 1)
    ).astype(F32)

    def trace(ref):
        total = jnp.zeros((tile, tile), F32)
        for _, cols in blocks:
            total = total + ref[cols, cols] * diag
        return jnp.sum(jnp.sum(total, axis=1, keepdims=True), axis=0, keepdims=True)

    def settle_gram(scale, centre):
        for rows, cols in blocks:
            part = e_gram[rows, cols]
            e_gram[rows, cols] = part if scale is None else part * scale
            e_gram[cols, cols] -= centre * diag
            gram[rows, cols] = e_gram[rows, cols].astype(BF16)
        mirror(gram, tile)

    def make_poly(d):
        p = NS_A + NS_B * d + NS_C * d * d
        for rows, cols in blocks:
            part = (NS_B + 2.0 * NS_C * d) * e_gram[rows, cols] + NS_C * nn(
                gram[rows, :], gram[:, cols]
            )
            e_poly[rows, cols] = part
            poly[rows, cols] = part.astype(BF16)
        mirror(poly, tile)
        return p

    def advance(d, p):
        for rows, cols in blocks:
            part = d * e_poly[rows, cols] + p * e_gram[rows, cols] + nn(gram[rows, :], poly[:, cols])
            e_half[rows, cols] = part
            half[rows, cols] = part.astype(BF16)
        mirror(half, tile)
        q = d * p
        for rows, cols in blocks:
            e_gram[rows, cols] = (
                q * e_poly[rows, cols] + p * e_half[rows, cols] + nn(half[rows, :], poly[:, cols])
            )
        centre = trace(e_gram) * (1.0 / width)
        settle_gram(None, centre)
        return q * p + centre

    def apply(p):
        now = x_own[...]
        return p * now + nn(now.astype(BF16), poly[...])

    for rows, cols in blocks:
        e_gram[rows, cols] = lax.fori_loop(
            0,
            x_ref.shape[0] // chunk,
            lambda r, acc: acc
            + tn(
                x_ref[pl.ds(pl.multiple_of(r * chunk, chunk), chunk), rows],
                x_ref[pl.ds(pl.multiple_of(r * chunk, chunk), chunk), cols],
            ),
            jnp.zeros((rows.stop, tile), F32),
        )
    square = trace(e_gram)
    inv = 1.0 / (jnp.sqrt(square) + 1e-07)
    first = square * inv * inv * (1.0 / width)
    settle_gram(inv * inv, first)
    rows = own // 4
    for k in range(4):
        block = x_ref[pl.ds(pl.multiple_of(start_ref[0, k], rows), rows), :]
        x_own[k * rows : (k + 1) * rows, :] = block.astype(F32) * inv

    def sweep(_, d):
        p = make_poly(d)
        x_own[...] = apply(p)
        return advance(d, p)

    d = lax.fori_loop(0, NS_STEPS - 1, sweep, first)
    o_ref[...] = apply(make_poly(d)).astype(BF16)


def orthogonal(pieces, firsts, own, *tokens):
    count = len(pieces)
    rows, width = count * pieces[0].shape[0], pieces[0].shape[1]
    wide = pltpu.VMEM((width, width), F32)
    low = pltpu.VMEM((width, width), BF16)
    return pl.pallas_call(
        functools.partial(schulz_kernel, count),
        out_shape=jax.ShapeDtypeStruct((own, width), BF16),
        in_specs=[SMEM_SPEC] + [HBM_SPEC] * (count + len(tokens)),
        out_specs=VMEM_SPEC,
        scratch_shapes=[
            pltpu.VMEM((rows, width), BF16),
            pltpu.VMEM((own, width), F32),
            wide,
            wide,
            wide,
            low,
            low,
            low,
            pltpu.SemaphoreType.DMA((count,)),
        ],
        compiler_params=pltpu.CompilerParams(vmem_limit_bytes=48 * 2**20),
        cost_estimate=pl.CostEstimate(
            flops=44 * 2**30, bytes_accessed=4 * rows * width, transcendentals=0
        ),
        name="schulz",
    )(firsts, *pieces, *tokens)


def on_device(
    n,
    tokens,
    cotangent,
    pair_order,
    norm_gains,
    head_gains,
    gate_head,
    w_query,
    w_keyval,
    w_outproj,
    w_gateup,
    w_down,
    mom_norm,
    mom_head,
    mom_gate_head,
    mom_query,
    mom_keyval,
    mom_outproj,
    mom_gateup,
    mom_down,
):
    quarter = n // 4
    my_h, my_m, my_i = lax.axis_index("h"), lax.axis_index("m"), lax.axis_index("i")
    my_b, my_c, my_x = lax.axis_index("b"), lax.axis_index("c"), lax.axis_index("x")
    me = lax.axis_index(ALL)
    everywhere = ("h", "m", "i")
    sub = my_c * 2 + my_b
    my_plane = my_h * 2 + my_m
    tok_dev, width = tokens.shape[1], tokens.shape[2]
    head_dim = head_gains.shape[1]
    scale = 1.0 / math.sqrt(head_dim)
    piece = tok_dev // 2
    group_rows = 8 * tok_dev

    rows_tok = swap_halves(tokens[0], my_h, my_x)
    xf = rows_tok.astype(F32)
    r1 = rms_scale(xf)
    y1 = xf * r1
    normed_rows = (y1 * norm_gains[0]).astype(BF16)
    q_rows = w_query.shape[0] // 4
    kv_rows = w_keyval.shape[1] // 4
    heads_here = q_rows // head_dim
    wgate = lax.dynamic_slice_in_dim(gate_head, (my_x * 4 + sub) * heads_here, heads_here, 0)
    gate_pad = 128 - heads_here
    small_block = w_keyval.shape[1] // (4 * n)
    out_block = w_outproj.shape[0] // (4 * n)
    ff_block = w_gateup.shape[1] // (4 * n)
    ff_rows = n * ff_block
    w_in, wo, wgu, wd = weight_slices(
        sub,
        w_query,
        w_keyval,
        w_outproj,
        w_gateup,
        w_down,
        jnp.pad(wgate, ((0, gate_pad), (0, 0))),
    )


    order_ids = jnp.arange(pair_order.shape[0], dtype=jnp.int32)

    def group_place(r_index):
        flips = jnp.arange(8, dtype=jnp.int32)
        dev_x = my_x ^ (flips & 1)
        dev_b = my_b ^ ((flips >> 1) & 1)
        dev_c = my_c ^ (flips >> 2)
        ctx_ids = ((dev_x * (n // 2) + r_index) * 2 + dev_b) * 2 + dev_c
        owner = jnp.sum(
            jnp.where(ctx_ids[:, None] == order_ids[None, :], pair_order[None, :], 0), axis=1
        )
        blocks = jnp.stack([owner, 2 * pair_order.shape[0] - 1 - owner], axis=1)
        spots = blocks[:, :, None] * piece + jnp.arange(piece, dtype=jnp.int32)
        return spots.reshape(group_rows)

    my_r = my_m * quarter + my_i
    place = group_place(my_r)
    if n == 4:
        key_place = jnp.concatenate([place, group_place(my_r ^ 1)])
    else:
        key_place = jnp.concatenate([group_place(r) for r in range(n // 2)])

    def gather_keys(v):
        if n == 4:
            return jnp.concatenate([v, flip(v, "m")], axis=0)
        return lax.all_gather(v, ("m", "i"), axis=0, tiled=True)

    def sum_keys(v):
        if n == 4:
            return v[:group_rows] + flip(v[group_rows:].astype(BF16), "m").astype(F32)
        return lax.psum_scatter(v, ("m", "i"), scatter_dimension=0, tiled=True)

    inverse = ROPE_BASE ** (-(2.0 * jnp.arange(head_dim // 2, dtype=F32)) / head_dim)
    angles = place.astype(F32)[:, None] * inverse[None, :]
    cosine, sine = jnp.cos(angles), jnp.sin(angles)
    normed_rows = tie(normed_rows, w_in, cosine, key_place)
    normed = gather_group(normed_rows)
    projected = nt(normed, w_in)
    rows_cot = swap_halves(held(cotangent[0], normed_rows), my_h, my_x)
    cot_near = gather_near(tie(rows_cot, projected))
    query_raw = jnp.stack(
        [projected[:, j * head_dim : (j + 1) * head_dim] for j in range(heads_here)]
    )
    key_raw = projected[:, q_rows : q_rows + kv_rows]
    value_rows = projected[:, q_rows + kv_rows : q_rows + 2 * kv_rows].astype(BF16)
    logits = projected[:, q_rows + 2 * kv_rows : q_rows + 2 * kv_rows + heads_here]
    rq, rk = rms_scale(query_raw), rms_scale(key_raw)
    yq, yk = query_raw * rq, key_raw * rk
    query_rows = rotate(yq * head_gains[0], cosine, sine).astype(BF16)
    key_rows = rotate(yk * head_gains[1], cosine, sine).astype(BF16)
    key_all, value_all = gather_keys(key_rows), gather_keys(value_rows)
    flat_query = query_rows.reshape(heads_here * group_rows, head_dim)
    flat_place = jnp.tile(place, heads_here)
    wide = jnp.concatenate([value_all, jnp.ones_like(value_all)], axis=1)
    summed, total = attend(flat_query, key_all, wide, flat_place, key_place, scale)
    attended = (summed / total).reshape(heads_here, group_rows, head_dim)
    total = total.reshape(heads_here, group_rows, 1)
    gate_sig = jax.nn.sigmoid(logits).T[:, :, None]
    gated = attended * gate_sig
    gated = jnp.concatenate([gated[j] for j in range(heads_here)], axis=1).astype(BF16)
    middle = xf + sum_group(nn(gated, wo))
    grad_all = gather_far(cot_near)
    r2 = rms_scale(middle)
    y2 = middle * r2
    hidden_in = gather_group((y2 * norm_gains[1]).astype(BF16))
    gate_up = nt(hidden_in, wgu)
    gate_part, up_part = gate_up[:, :ff_rows], gate_up[:, ff_rows:]
    sg = jax.nn.sigmoid(gate_part)
    silu = gate_part * sg
    hidden = (silu * up_part).astype(BF16)

    dhidden = nt(grad_all, wd)
    dgu = jnp.concatenate(
        [
            (dhidden * up_part * sg * (1.0 + gate_part * (1.0 - sg))).astype(BF16),
            (dhidden * silu).astype(BF16),
        ],
        axis=1,
    )
    grad_gu = tn(dgu, hidden_in).astype(BF16)
    grad_d = tn(hidden, grad_all).astype(BF16)
    ff_grad = lax.psum_scatter(
        jnp.concatenate([grad_d, jnp.zeros_like(grad_d), grad_gu], axis=0),
        ("h", "m", "i"),
        scatter_dimension=0,
        tiled=True,
    )
    dhn = sum_group(nn(dgu, wgu))
    gout = rows_cot.astype(F32)
    norm_terms_mid = jnp.sum(dhn * y2, axis=0)
    dmiddle = gout + norm_back(dhn, y2, r2, norm_gains[1])
    dbranch = gather_group(dmiddle.astype(BF16))

    first_moms = (mom_gateup, mom_down)
    first_places = ((GATE, UP), (DOWN,))
    second_moms = (mom_query, mom_keyval, mom_outproj)
    second_places = ((QUERY,), (KEY, VALUE), (OUT,))
    first_pack = pack(first_moms, first_places, ff_block, middle)
    second_pack = pack(second_moms, second_places, out_block, gate_up)
    first_old = to_home(first_pack, quarter, dhn)
    second_old = to_home(second_pack, quarter, dbranch)

    spot = me % (4 * n)
    mine_now, other_now = owned_rows(
        jnp.stack([spot, spot ^ 1]).reshape(1, 2),
        (w_query, w_keyval, w_outproj, w_gateup, w_down),
        n,
        dbranch,
    )
    old_rows = jnp.where(my_x == my_h, mine_now, flip(other_now, "x"))

    dgated = nt(dbranch, wo)
    def over_i(v):
        return lax.psum_scatter(v, "i", scatter_dimension=0, tiled=True) if quarter > 1 else v

    def to_out_plane(v):
        v = v.astype(F32) + lax.ppermute(v, ("h", "m"), [(0, 1), (3, 2)]).astype(F32)
        return v + lax.ppermute(v.astype(BF16), ("h", "m"), [(2, 1)]).astype(F32)

    def to_block(v):
        v = v.reshape(-1, width)
        return jnp.concatenate(
            [v]
            + [
                lax.ppermute(v, "i", [((j + d) % quarter, j) for j in range(quarter)])
                for d in range(1, quarter)
            ],
            axis=0,
        )

    def blend(old, grad):
        return (0.5 * old.astype(F32) + 0.5 * grad.astype(F32)).astype(BF16)

    def padded(v, rows, height):
        blocks = v.reshape(4, rows, width)
        return jnp.pad(blocks, ((0, 0), (0, height - rows), (0, 0)))

    position = my_b * 1 + my_i * 2
    source_b, source_i = position // quarter, position % quarter

    def firsts(rows, mine_first):
        return jnp.stack(
            [
                (
                    (((my_c ^ m) * 2 + (source_b ^ my_b)) * 2 + (my_x ^ h))
                    if mine_first
                    else (source_b * 2 + m) * 2 + h
                )
                * (4 * quarter * rows)
                + ((source_i - my_i) % quarter) * (4 * rows)
                + (my_c * 2 + my_x) * rows
                for h in range(2)
                for m in range(2)
            ]
        ).reshape(1, 4)

    grad_o = to_out_plane(over_i(tn(gated, dbranch).astype(BF16)))
    first_grad = ff_grad.reshape(4, ff_block, width)
    first_mine = blend(first_old, first_grad)
    out_sum = sum_core(nn(hidden, wd))

    dgated = jnp.stack([dgated[:, j * head_dim : (j + 1) * head_dim] for j in range(heads_here)])
    dattended = dgated * gate_sig
    dlogit = (
        gate_sig * (1.0 - gate_sig) * jnp.sum(dgated * attended, axis=-1, keepdims=True)
    ).astype(BF16)
    corr = jnp.sum(dattended * attended, axis=-1, keepdims=True) / total
    back_w = (dattended / total).astype(BF16)
    dquery, dkey_part, dvalue_part = attend_back(
        flat_query,
        back_w.reshape(heads_here * group_rows, head_dim),
        corr.reshape(heads_here * group_rows),
        key_all,
        value_all,
        flat_place,
        key_place,
        scale,
    )
    out_rows = middle + sum_near(out_sum)
    dkey_part = tie(dkey_part, out_rows)
    first_block = to_block(first_mine)
    first_start = lax.all_gather(first_block, ("b", "c", "x"), axis=0, tiled=True)
    dkey, dvalue = sum_keys(dkey_part), sum_keys(dvalue_part)
    dqn = rotate_back(dquery.reshape(heads_here, group_rows, head_dim), cosine, sine)
    dkn = rotate_back(dkey, cosine, sine)
    head_terms = jnp.stack([jnp.sum(dqn * yq, axis=(0, 1)), jnp.sum(dkn * yk, axis=0)])
    dq = norm_back(dqn, yq, rq, head_gains[0]).astype(BF16)
    dk = norm_back(dkn, yk, rk, head_gains[1]).astype(BF16)
    dall = jnp.concatenate(
        [dq[j] for j in range(heads_here)]
        + [dk, dvalue.astype(BF16)]
        + [dlogit[j] for j in range(heads_here)]
        + [jnp.zeros((group_rows, gate_pad), BF16)],
        axis=1,
    )
    dall = tie(dall, second_old, grad_o)
    grad_in = tn(dall, normed)
    query_part = grad_in[:q_rows].reshape(n, 2, small_block, width)
    second_part = jnp.concatenate(
        [
            jnp.transpose(query_part, (1, 0, 2, 3)).reshape(q_rows, width),
            grad_in[q_rows : q_rows + 2 * kv_rows],
        ],
        axis=0,
    ).astype(BF16)
    dnormed = sum_near(sum_core(nn(dall, w_in)))
    norm_terms_in = jnp.sum(dnormed * y1, axis=0)
    grad_rows = dmiddle + norm_back(dnormed, y1, r1, norm_gains[0])
    if quarter > 1:
        second_part = second_part.reshape(4, quarter, -1, width)
        second_part = lax.psum_scatter(second_part, "i", scatter_dimension=1, tiled=True)
    second_part = second_part.reshape(4, 4 * small_block, width)
    first_mid = turned(trade(first_grad, ("c", "x")))
    chunks = [
        lax.dynamic_index_in_dim(second_part, my_plane ^ k, 0, keepdims=False) for k in range(4)
    ]
    mine = chunks[0].astype(F32)
    for k, axes in ((1, ("m",)), (2, ("h",)), (3, ("h", "m"))):
        mine = mine + flip(chunks[k], *axes).astype(F32)
    mine = tie(mine.astype(BF16), first_mid, old_rows)
    pair = flip(mine, "m")
    mine, pair = (v.reshape(4, small_block, width) for v in (mine, pair))
    second_grad = jnp.concatenate(
        [mine, jnp.where(my_plane == QUERY, pair, jnp.zeros_like(pair))], axis=1
    )
    second_grad = jnp.where(
        my_plane == OUT, grad_o.astype(BF16).reshape(4, out_block, width), second_grad
    )
    second_block = to_block(blend(second_old, second_grad))
    small_z = sum_flips(
        jnp.concatenate(
            [
                lax.dynamic_update_slice_in_dim(
                    jnp.zeros((gate_head.shape[0], width), F32),
                    grad_in[q_rows + 2 * kv_rows : q_rows + 2 * kv_rows + heads_here],
                    (my_x * 4 + sub) * heads_here,
                    0,
                ),
                norm_terms_in[None],
                norm_terms_mid[None],
                jnp.pad(head_terms.reshape(1, 2 * head_dim), ((0, 0), (0, width - 2 * head_dim))),
            ],
            axis=0,
        ),
        (("m",), ("h",), ("h", "m")),
    )
    if quarter > 1:
        small_z = lax.psum(small_z, "i")
    second_near = gather_near(second_block)
    output = swap_halves(tie(out_rows.astype(BF16), dall), my_h, my_x)
    first_g = trade(tie(first_mid, second_block), ("h", "m"))
    if quarter > 1:
        first_g = lax.ppermute(first_g, ("i", "b"), fold_pairs(quarter))
    first_ortho = orthogonal(
        [first_start], firsts(ff_block, False), 4 * ff_block, second_block
    )
    second_ortho = orthogonal(
        pieces_far([tie(v, first_ortho) for v in second_near]), firsts(out_block, True), 4 * out_block, first_ortho
    )
    first_x = trade(first_ortho.reshape(4, ff_block, width), ("h", "m"))
    second_ortho = tie(second_ortho, first_x, first_g)
    second_x = trade(second_ortho.reshape(4, out_block, width), ("h", "m"))
    second_g = to_owner(tie(second_grad, first_ortho), quarter, second_ortho)


    grad_input = swap_halves(tie(grad_rows, first_ortho), my_h, my_x)

    head_count = gate_head.shape[0]
    small = sum_flips(tie(small_z, first_ortho), NEAR)
    small = sum_flips(tie(small, second_ortho), (("c",),))
    grad_gate = small[:head_count]
    grad_norm = small[head_count : head_count + 2]
    grad_head = small[head_count + 2, : 2 * head_dim].reshape(2, head_dim)
    new_mom_norm = 0.5 * mom_norm + 0.5 * grad_norm
    new_mom_head = 0.5 * mom_head + 0.5 * grad_head
    new_mom_gate = 0.5 * mom_gate_head + 0.5 * grad_gate
    new_norm = norm_gains - VECTOR_RATE * new_mom_norm
    new_head = head_gains - VECTOR_RATE * new_mom_head
    new_gate = gate_head.astype(F32) - VECTOR_RATE * new_mom_gate

    seq_len = tok_dev * n * 4
    out_boost = math.sqrt(width / max(1, 16384 // seq_len))
    rate = lambda rows: MATRIX_RATE * math.sqrt(rows * 8 * n)
    first_rates = {DOWN: rate(ff_block), GATE: rate(ff_block), UP: rate(ff_block)}
    second_rates = {
        QUERY: rate(out_block),
        OUT: out_boost * rate(out_block),
        KEY: rate(small_block),
        VALUE: rate(small_block),
    }
    q_at, k_at, v_at = 0, out_block, out_block + small_block
    o_at = v_at + small_block
    gate_at, up_at, down_at = (o_at + out_block + k * ff_block for k in range(3))
    g_gateup, g_down, m_gateup, m_down = settle(
        first_g, first_moms, first_moms, first_places, None
    )
    g_query, g_keyval, g_outproj, m_query, m_keyval, m_outproj = settle(
        second_g, second_moms, second_moms, second_places, None
    )
    n_gateup, n_down = settle(
        first_x,
        [old_rows],
        first_moms,
        (((GATE, gate_at), (UP, up_at)), ((DOWN, down_at),)),
        first_rates,
    )
    n_query, n_keyval, n_outproj = settle(
        second_x,
        [old_rows],
        second_moms,
        (((QUERY, q_at),), ((KEY, k_at), (VALUE, v_at)), ((OUT, o_at),)),
        second_rates,
    )

    return (
        output[None],
        grad_input[None],
        grad_norm,
        grad_head,
        grad_gate,
        g_query,
        g_keyval,
        g_outproj,
        g_gateup,
        g_down,
        new_mom_norm,
        new_mom_head,
        new_mom_gate,
        m_query,
        m_keyval,
        m_outproj,
        m_gateup,
        m_down,
        new_norm,
        new_head,
        new_gate,
        n_query,
        n_keyval,
        n_outproj,
        n_gateup,
        n_down,
    )


def solution(mesh):
    count = mesh.devices.size
    n = count // 8
    sizes = {"h": 2, "m": 2, "i": n // 4, "b": 2, "c": 2, "x": 2}
    fine = Mesh(mesh.devices.reshape(tuple(sizes[axis] for axis in ALL)), ALL)
    rows3 = P("x", CTX, None)
    own2 = P(ALL, None)
    own3 = P(None, ALL, None)
    half2 = P("x", None)
    half3 = P(None, "x", None)
    owners = (own2, own3, own2, own3, own2)
    return jax.shard_map(
        functools.partial(on_device, n),
        mesh=fine,
        in_specs=(rows3, rows3, P(), P(), P(), P(), half2, half3, half2, half3, half2)
        + (P(), P(), P())
        + owners,
        out_specs=(rows3, rows3, P(), P(), P())
        + owners
        + (P(), P(), P())
        + owners
        + (P(), P(), P())
        + owners,
        check_vma=False,
    )
```

```python
import functools
import math

import jax
import jax.numpy as jnp
from jax import lax
from jax.experimental import pallas as pl
from jax.experimental.pallas import tpu as pltpu
from jax.sharding import Mesh, PartitionSpec as P

NS_STEPS = 5
NORM_EPS = 1e-06
ROPE_BASE = 1000000.0
NS_A = 3.4445
NS_B = -4.775
NS_C = 2.0315
MATRIX_RATE = 0.03
VECTOR_RATE = 0.003
CTX = ("h", "m", "i", "b", "c")
ALL = CTX + ("x",)
F32 = jnp.float32
BF16 = jnp.bfloat16


def nt(p, q):
    return lax.dot_general(p, q, (((1,), (1,)), ((), ())), preferred_element_type=F32)


def nn(p, q):
    return lax.dot_general(p, q, (((1,), (0,)), ((), ())), preferred_element_type=F32)


def tn(p, q):
    return lax.dot_general(p, q, (((0,), (0,)), ((), ())), preferred_element_type=F32)


def flip(v, *axes):
    last = 2 ** len(axes) - 1
    return lax.ppermute(v, tuple(sorted(axes, key=ALL.index)), [(j, j ^ last) for j in range(last + 1)])


NEAR = (("x",), ("b",), ("b", "x"))


def gather_near(v):
    return [v] + [flip(v, *axes) for axes in NEAR]


def pieces_far(near):
    return near + [flip(member, "c") for member in near]


def join_kernel(*refs):
    ins, out, sems = refs[:-2], refs[-2], refs[-1]
    rows = ins[0].shape[0]
    run_copies([(ref, out.at[pl.ds(k * rows, rows)]) for k, ref in enumerate(ins)], sems)


def join(pieces):
    rows, width = pieces[0].shape
    count = len(pieces)
    return pl.pallas_call(
        join_kernel,
        out_shape=jax.ShapeDtypeStruct((count * rows, width), pieces[0].dtype),
        in_specs=[HBM_SPEC] * count,
        out_specs=VMEM_SPEC,
        scratch_shapes=[pltpu.SemaphoreType.DMA((count,))],
        compiler_params=SMALL,
        cost_estimate=pl.CostEstimate(
            flops=0, bytes_accessed=4 * count * rows * width, transcendentals=0
        ),
        name="join",
    )(*pieces)


def gather_far(near):
    return join(pieces_far(near))


def gather_group(v):
    return gather_far(gather_near(v))


def sum_core(part):
    half = part.shape[0] // 2
    return part[:half] + flip(part[half:].astype(BF16), "c").astype(F32)


def sum_near(part):
    rows = part.shape[0] // 4
    low = part.astype(BF16)
    total = part[:rows]
    for slot, axes in enumerate(NEAR, 1):
        total = total + flip(low[slot * rows : (slot + 1) * rows], *axes).astype(F32)
    return total


def sum_group(part):
    return sum_near(sum_core(part))


def sum_flips(v, flips):
    return sum((flip(v, *axes) for axes in flips), v)


def swap_halves(v, my_half, my_x):
    other = lax.ppermute(v, ("h", "x"), [(1, 2), (2, 1)])
    return jnp.where(my_half == my_x, v, other)


DOWN, NONE, GATE, UP = range(4)
QUERY, OUT, KEY, VALUE = range(4)

def trade(v, axes):
    return lax.all_to_all(v, axes, split_axis=0, concat_axis=0, tiled=True)


def turned(v):
    return jnp.stack([v[0], v[2], v[1], v[3]])


def fold_pairs(q):
    return [(i * 2 + b, b * q + i) for i in range(q) for b in range(2)]


VMEM_SPEC = pl.BlockSpec(memory_space=pltpu.VMEM)
SMEM_SPEC = pl.BlockSpec(memory_space=pltpu.SMEM)
SMALL = pltpu.CompilerParams(vmem_limit_bytes=32 * 2**20)
LARGE = pltpu.CompilerParams(vmem_limit_bytes=60 * 2**20)


HBM_SPEC = pl.BlockSpec(memory_space=pl.ANY)
FAR_SPEC = pl.BlockSpec(memory_space=pltpu.HBM)


def run_copies(pairs, sems):
    copies = [pltpu.make_async_copy(p, q, sems.at[k]) for k, (p, q) in enumerate(pairs)]
    for copy in copies:
        copy.start()
    for copy in copies:
        copy.wait()


def slices_kernel(sub_ref, wq, wkv, wo, wgu, wd, gate, w_in, o_out, gu_out, d_out, sems):
    sub = sub_ref[0, 0]
    q_rows, kv_rows = o_out.shape[0], wkv.shape[1] // 4

    def part(ref, rows):
        return ref.at[pl.ds(pl.multiple_of(sub * rows, rows), rows)]

    pairs = [
        (part(wq, q_rows), w_in.at[pl.ds(0, q_rows)]),
        (part(wkv.at[0], kv_rows), w_in.at[pl.ds(q_rows, kv_rows)]),
        (part(wkv.at[1], kv_rows), w_in.at[pl.ds(q_rows + kv_rows, kv_rows)]),
        (gate, w_in.at[pl.ds(q_rows + 2 * kv_rows, gate.shape[0])]),
        (part(wo, q_rows), o_out),
    ]
    pairs += [(part(wgu.at[g], d_out.shape[0]), gu_out.at[g]) for g in range(2)]
    pairs.append((part(wd, d_out.shape[0]), d_out))
    run_copies(pairs, sems)


def weight_slices(sub, w_query, w_keyval, w_outproj, w_gateup, w_down, gate):
    width = w_query.shape[1]
    q_rows, kv_rows = w_query.shape[0] // 4, w_keyval.shape[1] // 4
    ff_rows = w_down.shape[0] // 4
    w_in, wo, wgu, wd = pl.pallas_call(
        slices_kernel,
        out_shape=[
            jax.ShapeDtypeStruct((q_rows + 2 * kv_rows + gate.shape[0], width), BF16),
            jax.ShapeDtypeStruct((q_rows, width), BF16),
            jax.ShapeDtypeStruct((2, ff_rows, width), BF16),
            jax.ShapeDtypeStruct((ff_rows, width), BF16),
        ],
        in_specs=[SMEM_SPEC] + [FAR_SPEC] * 5 + [HBM_SPEC],
        out_specs=[VMEM_SPEC] * 4,
        scratch_shapes=[pltpu.SemaphoreType.DMA((8,))],
        compiler_params=LARGE,
        cost_estimate=pl.CostEstimate(flops=0, bytes_accessed=2**23, transcendentals=0),
        name="slices",
    )(
        sub.reshape(1, 1),
        w_query,
        w_keyval,
        w_outproj,
        w_gateup,
        w_down,
        gate,
    )
    return w_in, wo, wgu.reshape(2 * ff_rows, width), wd


def owned_kernel(spot_ref, *refs):
    ins, outs, sems = refs[:5], refs[-3:-1], refs[-1]
    pairs = []
    for k, out in enumerate(outs):
        spot, at = spot_ref[0, k], 0
        for ref in ins:
            rows = ref.shape[-2] // row_blocks(out, ins)
            span = pl.ds(pl.multiple_of(spot * rows, rows), rows)
            for part in [ref.at[j] for j in range(2)] if len(ref.shape) == 3 else [ref]:
                pairs.append((part.at[span], out.at[pl.ds(at, rows)]))
                at += rows
    run_copies(pairs, sems)


def row_blocks(out, ins):
    total = sum(ref.shape[-2] * (2 if len(ref.shape) == 3 else 1) for ref in ins)
    return total // out.shape[0]


def owned_rows(spots, weights, n, *tokens):
    rows = sum(w.shape[-2] * (2 if w.ndim == 3 else 1) for w in weights) // (4 * n)
    out = jax.ShapeDtypeStruct((rows, weights[0].shape[-1]), BF16)
    return pl.pallas_call(
        owned_kernel,
        out_shape=[out, out],
        in_specs=[SMEM_SPEC] + [FAR_SPEC] * 5 + [HBM_SPEC] * len(tokens),
        out_specs=[VMEM_SPEC] * 2,
        scratch_shapes=[pltpu.SemaphoreType.DMA((14,))],
        compiler_params=LARGE,
        cost_estimate=pl.CostEstimate(flops=0, bytes_accessed=2**22, transcendentals=0),
        name="owned",
    )(spots, *weights, *tokens)


def tie(value, *tokens):
    return pl.pallas_call(
        lambda *refs: None,
        out_shape=jax.ShapeDtypeStruct(value.shape, value.dtype),
        in_specs=[HBM_SPEC] * (1 + len(tokens)),
        out_specs=HBM_SPEC,
        input_output_aliases={0: 0},
        cost_estimate=pl.CostEstimate(flops=0, bytes_accessed=0, transcendentals=0),
        name="tie",
    )(value, *tokens)


def pack_kernel(places, ins, *refs):
    out = refs[-1]
    out[...] = jnp.zeros_like(out)
    for ref, item in zip(refs[:ins], places):
        rows = ref.shape[-2]
        for j, (member, first) in enumerate(item):
            source = ref[j] if len(ref.shape) == 3 else ref[...]
            out[member, first : first + rows] = source.astype(BF16)


def pack(arrays, places, height, *tokens):
    width = arrays[0].shape[-1]
    return pl.pallas_call(
        functools.partial(pack_kernel, places, len(arrays)),
        out_shape=jax.ShapeDtypeStruct((4, height, width), BF16),
        in_specs=[VMEM_SPEC] * len(arrays) + [HBM_SPEC] * len(tokens),
        out_specs=VMEM_SPEC,
        compiler_params=SMALL,
        cost_estimate=pl.CostEstimate(flops=0, bytes_accessed=24 * height * width, transcendentals=0),
        name="pack",
    )(*arrays, *tokens)


def held_kernel(v_ref, *refs):
    refs[-1][...] = v_ref[...]


def held(v, *tokens):
    return pl.pallas_call(
        held_kernel,
        out_shape=jax.ShapeDtypeStruct(v.shape, v.dtype),
        in_specs=[VMEM_SPEC] + [HBM_SPEC] * len(tokens),
        out_specs=VMEM_SPEC,
        compiler_params=SMALL,
        cost_estimate=pl.CostEstimate(flops=0, bytes_accessed=4 * v.size, transcendentals=0),
        name="held",
    )(v, *tokens)


def settle_kernel(places, rates, items, *refs):
    if rates is None:
        count = len(places)
        olds, outs = refs[:count], refs[count:]
    else:
        old_ref, outs = refs[0], refs[1:]
    for a, item in enumerate(places):
        rows = outs[a].shape[-2]
        for j, place in enumerate(item):
            at = (j,) if len(outs[a].shape) == 3 else (slice(None),)
            member, first = place if rates is not None else (place, 0)
            value = items[member, :rows].astype(F32)
            if rates is None:
                outs[a][at] = value
                outs[count + a][at] = 0.5 * olds[a][at] + 0.5 * value
            else:
                old = old_ref[first : first + rows, :].astype(F32)
                outs[a][at] = old - rates[member] * value


def settle(items, olds, shapes, places, rates):
    shapes = [jax.ShapeDtypeStruct(v.shape, F32) for v in shapes]
    shapes = shapes * (2 if rates is None else 1)
    return pl.pallas_call(
        functools.partial(settle_kernel, places, rates),
        out_shape=shapes,
        in_specs=[VMEM_SPEC] * (1 + len(olds)),
        out_specs=[VMEM_SPEC] * len(shapes),
        compiler_params=SMALL,
        cost_estimate=pl.CostEstimate(flops=0, bytes_accessed=12 * items.size, transcendentals=0),
        name="settle",
    )(items, *olds)


TILE = 512
ATTENTION = pltpu.CompilerParams(vmem_limit_bytes=44 * 2**20)


def tile_at(j, size=TILE, offset=0):
    return pl.ds(pl.multiple_of(j * size + offset, size), size)


def shape_of(dtype, *shape):
    return jax.ShapeDtypeStruct(shape, dtype)


def cost(microseconds):
    return pl.CostEstimate(
        flops=int(microseconds * 1.15e9), bytes_accessed=2**20, transcendentals=0
    )


def head_scale(raw):
    return lax.rsqrt(jnp.mean(raw * raw, axis=-1, keepdims=True) + NORM_EPS)


def head_back(grad, raw, cosine, sine, gain):
    grad = grad * cosine - pltpu.roll(grad, grad.shape[1] // 2, 1) * sine
    scale = head_scale(raw)
    unit = raw * scale
    pushed = grad * gain
    back = scale * (pushed - unit * jnp.mean(pushed * unit, axis=-1, keepdims=True))
    return back, jnp.sum(grad * unit, axis=0, keepdims=True)


def project_kernel(heads, n_ref, w_ref, cos_ref, sin_ref, gain_ref, q_ref, kv_ref, lg_ref, raw_ref):
    rows, dim = n_ref.shape[0], cos_ref.shape[1]

    @pl.loop(0, rows // 256)
    def _(t):
        span = tile_at(t, 256)
        out = nt(n_ref[span, :], w_ref[...])
        cosine, sine = cos_ref[span, :], sin_ref[span, :]
        for j in range(heads + 1):
            raw = out[:, j * dim : (j + 1) * dim]
            raw_ref[j, span, :] = raw
            which = slice(0, 1) if j < heads else slice(1, 2)
            unit = raw * head_scale(raw) * gain_ref[which, :]
            turned_rows = unit * cosine + pltpu.roll(unit, dim // 2, 1) * sine
            if j < heads:
                q_ref[j, span, :] = turned_rows.astype(BF16)
            else:
                kv_ref[0, span, :] = turned_rows.astype(BF16)
        kv_ref[1, span, :] = out[:, (heads + 1) * dim : (heads + 2) * dim].astype(BF16)
        lg_ref[span, :] = jax.nn.sigmoid(out[:, (heads + 2) * dim : (heads + 3) * dim])


def project(normed, w_in, cosine, sine, gains):
    rows, dim = cosine.shape
    heads = w_in.shape[0] // dim - 3
    return pl.pallas_call(
        functools.partial(project_kernel, heads),
        out_shape=[
            shape_of(BF16, heads, rows, dim),
            shape_of(BF16, 2, rows, dim),
            shape_of(F32, rows, dim),
            shape_of(F32, heads + 1, rows, dim),
        ],
        in_specs=[VMEM_SPEC] * 5,
        out_specs=[VMEM_SPEC] * 4,
        compiler_params=ATTENTION,
        cost_estimate=cost(6),
        name="project",
    )(normed, w_in, cosine, sine, gains)


def widened(values):
    return jnp.concatenate([values, jnp.ones_like(values)], axis=1)


def attend_kernel(scale, q_ref, lg_ref, qp_ref, kp_ref, *refs):
    pieces, (att_ref, tot_ref, gated_ref) = refs[:-3], refs[-3:]
    heads, rows, dim = q_ref.shape
    for h in range(heads):

        @pl.loop(0, rows // TILE)
        def _(i):
            span = tile_at(i)
            query, place = q_ref[h, span, :], qp_ref[span, :]
            total = jnp.zeros((TILE, 2 * dim), F32)
            for number, kv_ref in enumerate(pieces):
                offset = number * kv_ref.shape[1]

                def step(j, acc, kv_ref=kv_ref, offset=offset):
                    scores = nt(query, kv_ref[0, tile_at(j), :])
                    seen = kp_ref[:, tile_at(j, offset=offset)] <= place
                    weights = jnp.where(seen, jnp.exp2(scores * scale), 0.0)
                    return acc + nn(weights.astype(BF16), widened(kv_ref[1, tile_at(j), :]))

                total = lax.fori_loop(0, kv_ref.shape[1] // TILE, step, total)
            weight = total[:, dim : dim + 1]
            attended = total[:, :dim] / weight
            att_ref[h, span, :] = attended
            tot_ref[h, span, :] = weight
            gated_ref[span, h * dim : (h + 1) * dim] = (
                attended * lg_ref[span, h : h + 1]
            ).astype(BF16)


def attend(query, sigmoids, pieces, q_place, k_place, scale, *tokens):
    heads, rows, dim = query.shape
    count = len(pieces)
    kernel = functools.partial(attend_kernel, scale * math.log2(math.e))

    def without_tokens(*refs):
        kernel(*refs[: 4 + count], *refs[4 + count + len(tokens) :])

    return pl.pallas_call(
        without_tokens,
        out_shape=[
            shape_of(F32, heads, rows, dim),
            shape_of(F32, heads, rows, 1),
            shape_of(BF16, rows, heads * dim),
        ],
        in_specs=[VMEM_SPEC] * (4 + count) + [HBM_SPEC] * len(tokens),
        out_specs=[VMEM_SPEC] * 3,
        compiler_params=ATTENTION,
        cost_estimate=cost(12),
        name="attend",
    )(query, sigmoids, q_place[:, None], k_place[None, :], *pieces, *tokens)


def before_kernel(b_ref, w_ref, att_ref, tot_ref, lg_ref, bw_ref, dl_ref):
    heads, rows, dim = att_ref.shape
    lanes = lax.broadcasted_iota(jnp.int32, (256, dim), 1)

    @pl.loop(0, rows // 256)
    def _(t):
        span = tile_at(t, 256)
        grad = nt(b_ref[span, :], w_ref[...])
        logits = jnp.zeros((256, dim), F32)
        for h in range(heads):
            part = grad[:, h * dim : (h + 1) * dim]
            sig = lg_ref[span, h : h + 1]
            total = tot_ref[h, span, :]
            along = jnp.sum(part * att_ref[h, span, :], axis=-1, keepdims=True)
            logits = jnp.where(lanes == h, sig * (1.0 - sig) * along, logits)
            bw_ref[h, span, :dim] = (part * (sig / total)).astype(BF16)
            corr = -sig * along / total
            high = corr.astype(BF16).astype(F32)
            extra = jnp.where(lanes == 0, high, jnp.where(lanes == 1, corr - high, 0.0))
            bw_ref[h, span, dim:] = extra.astype(BF16)
        dl_ref[span, :] = logits.astype(BF16)


def before_attention(dbranch, wo, attended, total, sigmoids):
    heads, rows, dim = attended.shape
    return pl.pallas_call(
        before_kernel,
        out_shape=[shape_of(BF16, heads, rows, 2 * dim), shape_of(BF16, rows, dim)],
        in_specs=[VMEM_SPEC] * 5,
        out_specs=[VMEM_SPEC] * 2,
        compiler_params=ATTENTION,
        cost_estimate=cost(5),
        name="before",
    )(dbranch, wo, attended, total, sigmoids)


def attend_back_kernel(
    scale, count, q_ref, bw_ref, raw_ref, cos_ref, sin_ref, gain_ref, qp_ref, kp_ref, *refs
):
    pieces = refs[:count]
    dq_ref, terms_ref = refs[count : count + 2]
    outs, sums = refs[count + 2 : 2 * count + 2], refs[2 * count + 2 :]
    heads, rows, dim = q_ref.shape
    grow = scale * math.log2(math.e)
    for ref in sums:
        ref[...] = jnp.zeros_like(ref)
    terms_ref[...] = jnp.zeros_like(terms_ref)
    for h in range(heads):

        @pl.loop(0, rows // TILE)
        def _(i):
            span = tile_at(i)
            query, back, place = q_ref[h, span, :], bw_ref[h, span, :], qp_ref[:, span]
            total = jnp.zeros((TILE, dim), F32)
            for number, (kv_ref, sum_ref) in enumerate(zip(pieces, sums)):
                offset = number * kv_ref.shape[1]

                def step(j, acc, kv_ref=kv_ref, sum_ref=sum_ref, offset=offset):
                    keys = tile_at(j)
                    key = kv_ref[0, keys, :]
                    seen = kp_ref[tile_at(j, offset=offset), :] <= place
                    weights = jnp.where(seen, jnp.exp2(nt(key, query) * grow), 0.0)
                    push = nt(widened(kv_ref[1, keys, :]), back)
                    dscore = (weights * push * scale).astype(BF16)
                    sum_ref[1, keys, :] += nn(weights.astype(BF16), back[:, :dim])
                    sum_ref[0, keys, :] += nn(dscore, query)
                    return acc + tn(dscore, key)

                total = lax.fori_loop(0, kv_ref.shape[1] // TILE, step, total)
            grad, terms = head_back(
                total, raw_ref[h, span, :], cos_ref[span, :], sin_ref[span, :], gain_ref[0:1, :]
            )
            dq_ref[span, h * dim : (h + 1) * dim] = grad.astype(BF16)
            terms_ref[...] += terms

    for out, ref in zip(outs, sums):
        out[...] = ref[...].astype(out.dtype)


def attend_back(query, back, raw, cosine, sine, gains, pieces, q_place, k_place, scale):
    heads, rows, dim = query.shape
    count = len(pieces)
    return pl.pallas_call(
        functools.partial(attend_back_kernel, scale, count),
        out_shape=[shape_of(BF16, rows, heads * dim), shape_of(F32, 1, dim)]
        + [shape_of(BF16 if k else F32, *piece.shape) for k, piece in enumerate(pieces)],
        in_specs=[VMEM_SPEC] * (8 + count),
        out_specs=[VMEM_SPEC] * (2 + count),
        scratch_shapes=[pltpu.VMEM(piece.shape, F32) for piece in pieces],
        compiler_params=ATTENTION,
        cost_estimate=cost(18),
        name="attend_back",
    )(
        query, back, raw, cosine, sine, gains, q_place[None, :], k_place[:, None], *pieces
    )


def keys_kernel(own_ref, far_ref, raw_ref, cos_ref, sin_ref, gain_ref, dl_ref, out_ref, terms_ref):
    rows, dim = cos_ref.shape
    terms_ref[...] = jnp.zeros_like(terms_ref)

    @pl.loop(0, rows // 256)
    def _(t):
        span = tile_at(t, 256)
        both = [own_ref[k, span, :] + far_ref[k, span, :].astype(F32) for k in range(2)]
        grad, terms = head_back(
            both[0], raw_ref[raw_ref.shape[0] - 1, span, :], cos_ref[span, :], sin_ref[span, :], gain_ref[1:2, :]
        )
        terms_ref[...] += terms
        out_ref[span, :dim] = grad.astype(BF16)
        out_ref[span, dim : 2 * dim] = both[1].astype(BF16)
        out_ref[span, 2 * dim :] = dl_ref[span, :]


def keys_back(own, far, raw, cosine, sine, gains, dlogit):
    rows, dim = cosine.shape
    return pl.pallas_call(
        keys_kernel,
        out_shape=[shape_of(BF16, rows, 3 * dim), shape_of(F32, 1, dim)],
        in_specs=[VMEM_SPEC] * 7,
        out_specs=[VMEM_SPEC] * 2,
        compiler_params=ATTENTION,
        cost_estimate=cost(3),
        name="keys",
    )(own, far, raw, cosine, sine, gains, dlogit)


def rms_scale(v):
    return lax.rsqrt(jnp.mean(v * v, axis=-1, keepdims=True) + NORM_EPS)


def norm_back(grad, scaled, rscale, gains):
    pushed = grad * gains
    return rscale * (pushed - scaled * jnp.mean(pushed * scaled, axis=-1, keepdims=True))


def mirror(ref, tile):
    for j in range(ref.shape[0] // tile):
        for i in range(j):
            block = ref[i * tile : (i + 1) * tile, j * tile : (j + 1) * tile].astype(F32)
            ref[j * tile : (j + 1) * tile, i * tile : (i + 1) * tile] = block.T.astype(BF16)


def schulz_kernel(count, start_ref, *refs):
    pieces = refs[:count]
    o_ref, x_ref, x_own, e_gram, e_poly, e_half, gram, poly, half, sems = refs[-10:]
    piece = pieces[0].shape[0]
    copies = [
        pltpu.make_async_copy(ref, x_ref.at[pl.ds(k * piece, piece)], sems.at[k])
        for k, ref in enumerate(pieces)
    ]
    for copy in copies:
        copy.start()
    for copy in copies:
        copy.wait()
    chunk = min(1024, x_ref.shape[0])
    width = x_ref.shape[1]
    own = o_ref.shape[0]
    tile = 256
    blocks = [(slice(0, (j + 1) * tile), slice(j * tile, (j + 1) * tile)) for j in range(width // tile)]
    diag = (
        lax.broadcasted_iota(jnp.int32, (tile, tile), 0)
        == lax.broadcasted_iota(jnp.int32, (tile, tile), 1)
    ).astype(F32)

    def trace(ref):
        total = jnp.zeros((tile, tile), F32)
        for _, cols in blocks:
            total = total + ref[cols, cols] * diag
        return jnp.sum(jnp.sum(total, axis=1, keepdims=True), axis=0, keepdims=True)

    def settle_gram(scale, centre):
        for rows, cols in blocks:
            part = e_gram[rows, cols]
            e_gram[rows, cols] = part if scale is None else part * scale
            e_gram[cols, cols] -= centre * diag
            gram[rows, cols] = e_gram[rows, cols].astype(BF16)
        mirror(gram, tile)

    def make_poly(d):
        p = NS_A + NS_B * d + NS_C * d * d
        for rows, cols in blocks:
            part = (NS_B + 2.0 * NS_C * d) * e_gram[rows, cols] + NS_C * nn(
                gram[rows, :], gram[:, cols]
            )
            e_poly[rows, cols] = part
            poly[rows, cols] = part.astype(BF16)
        mirror(poly, tile)
        return p

    def advance(d, p):
        for rows, cols in blocks:
            part = d * e_poly[rows, cols] + p * e_gram[rows, cols] + nn(gram[rows, :], poly[:, cols])
            e_half[rows, cols] = part
            half[rows, cols] = part.astype(BF16)
        mirror(half, tile)
        q = d * p
        for rows, cols in blocks:
            e_gram[rows, cols] = (
                q * e_poly[rows, cols] + p * e_half[rows, cols] + nn(half[rows, :], poly[:, cols])
            )
        centre = trace(e_gram) * (1.0 / width)
        settle_gram(None, centre)
        return q * p + centre

    def apply(p):
        now = x_own[...]
        return p * now + nn(now.astype(BF16), poly[...])

    for rows, cols in blocks:
        e_gram[rows, cols] = lax.fori_loop(
            0,
            x_ref.shape[0] // chunk,
            lambda r, acc: acc
            + tn(
                x_ref[pl.ds(pl.multiple_of(r * chunk, chunk), chunk), rows],
                x_ref[pl.ds(pl.multiple_of(r * chunk, chunk), chunk), cols],
            ),
            jnp.zeros((rows.stop, tile), F32),
        )
    square = trace(e_gram)
    inv = 1.0 / (jnp.sqrt(square) + 1e-07)
    first = square * inv * inv * (1.0 / width)
    settle_gram(inv * inv, first)
    x_own[...] = x_ref[pl.ds(pl.multiple_of(start_ref[0, 0], own), own), :].astype(F32) * inv

    def sweep(_, d):
        p = make_poly(d)
        x_own[...] = apply(p)
        return advance(d, p)

    d = lax.fori_loop(0, NS_STEPS - 1, sweep, first)
    o_ref[...] = apply(make_poly(d)).astype(BF16)


def orthogonal(pieces, firsts, own, *tokens):
    count = len(pieces)
    rows, width = count * pieces[0].shape[0], pieces[0].shape[1]
    wide = pltpu.VMEM((width, width), F32)
    low = pltpu.VMEM((width, width), BF16)
    return pl.pallas_call(
        functools.partial(schulz_kernel, count),
        out_shape=jax.ShapeDtypeStruct((own, width), BF16),
        in_specs=[SMEM_SPEC] + [HBM_SPEC] * (count + len(tokens)),
        out_specs=VMEM_SPEC,
        scratch_shapes=[
            pltpu.VMEM((rows, width), BF16),
            pltpu.VMEM((own, width), F32),
            wide,
            wide,
            wide,
            low,
            low,
            low,
            pltpu.SemaphoreType.DMA((count,)),
        ],
        compiler_params=pltpu.CompilerParams(vmem_limit_bytes=48 * 2**20),
        cost_estimate=pl.CostEstimate(
            flops=44 * 2**30, bytes_accessed=4 * rows * width, transcendentals=0
        ),
        name="schulz",
    )(firsts, *pieces, *tokens)


def on_device(
    n,
    tokens,
    cotangent,
    pair_order,
    norm_gains,
    head_gains,
    gate_head,
    w_query,
    w_keyval,
    w_outproj,
    w_gateup,
    w_down,
    mom_norm,
    mom_head,
    mom_gate_head,
    mom_query,
    mom_keyval,
    mom_outproj,
    mom_gateup,
    mom_down,
):
    quarter = n // 4
    my_h, my_m, my_i = lax.axis_index("h"), lax.axis_index("m"), lax.axis_index("i")
    my_b, my_c, my_x = lax.axis_index("b"), lax.axis_index("c"), lax.axis_index("x")
    me = lax.axis_index(ALL)
    everywhere = ("h", "m", "i")
    sub = my_c * 2 + my_b
    my_plane = my_h * 2 + my_m
    tok_dev, width = tokens.shape[1], tokens.shape[2]
    head_dim = head_gains.shape[1]
    scale = 1.0 / math.sqrt(head_dim)
    piece = tok_dev // 2
    group_rows = 8 * tok_dev

    rows_tok = swap_halves(tokens[0], my_h, my_x)
    xf = rows_tok.astype(F32)
    r1 = rms_scale(xf)
    y1 = xf * r1
    normed_rows = (y1 * norm_gains[0]).astype(BF16)
    q_rows = w_query.shape[0] // 4
    kv_rows = w_keyval.shape[1] // 4
    heads_here = q_rows // head_dim
    wgate = lax.dynamic_slice_in_dim(gate_head, (my_x * 4 + sub) * heads_here, heads_here, 0)
    gate_pad = 128 - heads_here
    small_block = w_keyval.shape[1] // (4 * n)
    out_block = w_outproj.shape[0] // (4 * n)
    ff_block = w_gateup.shape[1] // (4 * n)
    ff_rows = n * ff_block
    w_in, wo, wgu, wd = weight_slices(
        sub,
        w_query,
        w_keyval,
        w_outproj,
        w_gateup,
        w_down,
        jnp.pad(wgate, ((0, gate_pad), (0, 0))),
    )


    order_ids = jnp.arange(pair_order.shape[0], dtype=jnp.int32)

    def group_place(r_index):
        flips = jnp.arange(8, dtype=jnp.int32)
        dev_x = my_x ^ (flips & 1)
        dev_b = my_b ^ ((flips >> 1) & 1)
        dev_c = my_c ^ (flips >> 2)
        ctx_ids = ((dev_x * (n // 2) + r_index) * 2 + dev_b) * 2 + dev_c
        owner = jnp.sum(
            jnp.where(ctx_ids[:, None] == order_ids[None, :], pair_order[None, :], 0), axis=1
        )
        blocks = jnp.stack([owner, 2 * pair_order.shape[0] - 1 - owner], axis=1)
        spots = blocks[:, :, None] * piece + jnp.arange(piece, dtype=jnp.int32)
        return spots.reshape(group_rows)

    my_r = my_m * quarter + my_i
    place = group_place(my_r)
    if n == 4:
        key_place = jnp.concatenate([place, group_place(my_r ^ 1)])
    else:
        key_place = jnp.concatenate([group_place(r) for r in range(n // 2)])

    def key_pieces(kv):
        if n == 4:
            return [kv, flip(kv, "m")]
        return [lax.all_gather(kv, ("m", "i"), axis=1, tiled=True)]

    def key_sums(parts):
        if n == 4:
            return parts[0], flip(parts[1], "m")
        mine = lax.psum_scatter(parts[0], ("m", "i"), scatter_dimension=1, tiled=True)
        return mine, jnp.zeros(mine.shape, BF16)

    half = head_dim // 2
    inverse = ROPE_BASE ** (-(2.0 * jnp.arange(half, dtype=F32)) / head_dim)
    angles = place.astype(F32)[:, None] * inverse[None, :]
    cosine, sine = jnp.cos(angles), jnp.sin(angles)
    cosine = jnp.concatenate([cosine, cosine], axis=1)
    sine = jnp.concatenate([-sine, sine], axis=1)
    normed_rows = tie(normed_rows, w_in, cosine, sine, key_place)
    normed = gather_group(normed_rows)
    query_rows, kv_rows_here, sigmoids, raw = project(normed, w_in, cosine, sine, head_gains)
    rows_cot = swap_halves(held(cotangent[0], w_in, cosine), my_h, my_x)
    kv_all = key_pieces(kv_rows_here)
    cot_near = gather_near(tie(rows_cot, query_rows))
    attended, total, gated = attend(
        query_rows, sigmoids, kv_all, place, key_place, scale, rows_cot
    )
    gated = tie(gated, *cot_near)

    first_moms = (mom_gateup, mom_down)
    first_places = ((GATE, UP), (DOWN,))
    second_moms = (mom_query, mom_keyval, mom_outproj)
    second_places = ((QUERY,), (KEY, VALUE), (OUT,))
    old_items = pack(
        first_moms + second_moms,
        [[(member, 0) for member in place] for place in first_places]
        + [[(member, ff_block) for member in place] for place in second_places],
        ff_block + out_block,
        query_rows,
    )
    if quarter > 1:
        old_items = lax.ppermute(old_items, ("i", "b"), [(d, p) for p, d in fold_pairs(quarter)])
    old_items = trade(old_items, ("h", "m"))

    middle = xf + sum_group(nn(gated, wo))
    grad_all = gather_far(cot_near)
    r2 = rms_scale(middle)
    y2 = middle * r2
    hidden_in = gather_group((y2 * norm_gains[1]).astype(BF16))
    gate_up = nt(hidden_in, wgu)
    gate_part, up_part = gate_up[:, :ff_rows], gate_up[:, ff_rows:]
    sg = jax.nn.sigmoid(gate_part)
    silu = gate_part * sg
    hidden = (silu * up_part).astype(BF16)

    dhidden = nt(grad_all, wd)
    dgu = jnp.concatenate(
        [
            (dhidden * up_part * sg * (1.0 + gate_part * (1.0 - sg))).astype(BF16),
            (dhidden * silu).astype(BF16),
        ],
        axis=1,
    )
    dgu = tie(dgu, old_items)
    grad_gu = tn(dgu, hidden_in).astype(BF16)
    grad_d = tn(hidden, grad_all).astype(BF16)
    ff_grad = lax.psum_scatter(
        jnp.concatenate([grad_d, jnp.zeros_like(grad_d), grad_gu], axis=0),
        ("h", "m", "i"),
        scatter_dimension=0,
        tiled=True,
    )
    dhn = sum_group(nn(dgu, wgu))
    gout = rows_cot.astype(F32)
    norm_terms_mid = jnp.sum(dhn * y2, axis=0)
    dmiddle = gout + norm_back(dhn, y2, r2, norm_gains[1])
    out_sum = sum_core(nn(hidden, wd))
    dbranch = gather_group(tie(dmiddle.astype(BF16), out_sum))

    back_w, dlogit = before_attention(dbranch, wo, attended, total, sigmoids)

    def over_i(v):
        return lax.psum_scatter(v, "i", scatter_dimension=0, tiled=True) if quarter > 1 else v

    def blend(old, grad):
        return (0.5 * old.astype(F32) + 0.5 * grad.astype(F32)).astype(BF16)

    def padded(v, rows, height):
        blocks = v.reshape(4, rows, width)
        return jnp.pad(blocks, ((0, 0), (0, height - rows), (0, 0)))

    everyone = ("i", "b", "c", "x")
    mine_at = lax.axis_index(everyone)

    grad_o = over_i(tn(gated, dbranch).astype(BF16))
    grad_o = grad_o.astype(F32) + lax.ppermute(grad_o, ("h", "m"), [(0, 1), (3, 2)]).astype(F32)
    first_grad = ff_grad.reshape(4, ff_block, width)
    out_sum = tie(out_sum, back_w)

    dq, query_terms, *kv_sums = attend_back(
        query_rows, back_w, raw, cosine, sine, head_gains, kv_all, place, key_place, scale
    )
    out_rows = middle + sum_near(out_sum)
    first_mid = turned(trade(tie(first_grad, dq), ("c", "x")))
    kv_sums[0] = tie(kv_sums[0], out_rows)
    first_old, second_old = old_items[:, :ff_block], old_items[:, ff_block:]
    first_block = blend(first_old, first_mid).reshape(4 * ff_block, width)
    first_start = lax.all_gather(first_block, everyone, axis=0, tiled=True)
    kv_own, kv_far = key_sums(kv_sums)
    dkv, key_terms = keys_back(kv_own, kv_far, raw, cosine, sine, head_gains, dlogit)
    grad_o = tie(grad_o, dkv)
    grad_o = grad_o + lax.ppermute(grad_o.astype(BF16), ("h", "m"), [(2, 1)]).astype(F32)
    head_terms = jnp.concatenate([query_terms, key_terms], axis=0)
    grad_q, grad_kv = tn(dq, normed), tn(dkv, normed)
    query_part = grad_q.reshape(n, 2, small_block, width)
    second_part = jnp.concatenate(
        [
            jnp.transpose(query_part, (1, 0, 2, 3)).reshape(q_rows, width),
            grad_kv[: 2 * kv_rows],
        ],
        axis=0,
    ).astype(BF16)
    dn_core = sum_core(nn(dq, w_in[:q_rows]) + nn(dkv, w_in[q_rows:]))
    dnormed = sum_near(dn_core)
    norm_terms_in = jnp.sum(dnormed * y1, axis=0)
    grad_rows = dmiddle + norm_back(dnormed, y1, r1, norm_gains[0])
    if quarter > 1:
        second_part = second_part.reshape(4, quarter, -1, width)
        second_part = lax.psum_scatter(second_part, "i", scatter_dimension=1, tiled=True)
    second_part = second_part.reshape(4, 4 * small_block, width)
    chunks = [
        lax.dynamic_index_in_dim(second_part, my_plane ^ k, 0, keepdims=False) for k in range(4)
    ]
    mine = chunks[0].astype(F32)
    for k, axes in ((1, ("m",)), (2, ("h",)), (3, ("h", "m"))):
        mine = mine + flip(chunks[k], *axes).astype(F32)
    mine = tie(mine.astype(BF16), dn_core)
    mine_sum = mine
    pair = flip(mine, "m")
    mine, pair = (v.reshape(4, small_block, width) for v in (mine, pair))
    second_grad = jnp.concatenate(
        [mine, jnp.where(my_plane == QUERY, pair, jnp.zeros_like(pair))], axis=1
    )
    second_grad = jnp.where(
        my_plane == OUT, grad_o.astype(BF16).reshape(4, out_block, width), second_grad
    )
    second_mid = turned(trade(second_grad, ("c", "x")))
    second_block = blend(second_old, second_mid).reshape(4 * out_block, width)
    small_z = (
        jnp.concatenate(
            [
                lax.dynamic_update_slice_in_dim(
                    jnp.zeros((gate_head.shape[0], width), F32),
                    grad_kv[2 * kv_rows : 2 * kv_rows + heads_here],
                    (my_x * 4 + sub) * heads_here,
                    0,
                ),
                norm_terms_in[None],
                norm_terms_mid[None],
                jnp.pad(head_terms.reshape(1, 2 * head_dim), ((0, 0), (0, width - 2 * head_dim))),
            ],
            axis=0,
        )
    )
    small = sum_flips(small_z, (("m",), ("h",), ("h", "m")))
    if quarter > 1:
        small = lax.psum(small, "i")
    small = sum_flips(small, NEAR)
    output = swap_halves(tie(out_rows.astype(BF16), mine_sum), my_h, my_x)
    second_block = tie(second_block, small, output)
    second_start = lax.all_gather(second_block, everyone, axis=0, tiled=True)
    spot = me % (4 * n)
    mine_now, other_now = owned_rows(
        jnp.stack([spot, spot ^ 1]).reshape(1, 2),
        (w_query, w_keyval, w_outproj, w_gateup, w_down),
        n,
        second_block,
    )
    first_g = trade(tie(first_mid, second_block), ("h", "m"))
    if quarter > 1:
        first_g = lax.ppermute(first_g, ("i", "b"), fold_pairs(quarter))
    first_ortho = orthogonal(
        [first_start], (mine_at * (4 * ff_block)).reshape(1, 1), 4 * ff_block, other_now
    )
    second_ortho = orthogonal([second_start], (mine_at * (4 * out_block)).reshape(1, 1), 4 * out_block, first_ortho)
    sent = lax.ppermute(tie(grad_rows.astype(BF16), other_now), ("h", "x"), [(1, 2), (2, 1)])
    grad_input = jnp.where(my_h == my_x, grad_rows, sent.astype(F32))
    returned = jnp.concatenate(
        [first_ortho.reshape(4, ff_block, width), tie(second_mid, first_ortho)], axis=1
    )
    returned = trade(tie(returned, first_g, sent), ("h", "m"))
    if quarter > 1:
        returned = lax.ppermute(returned, ("i", "b"), fold_pairs(quarter))
    first_x, second_g = returned[:, :ff_block], returned[:, ff_block:]
    old_rows = jnp.where(my_x == my_h, mine_now, flip(tie(other_now, first_ortho), "x"))
    second_ortho = tie(second_ortho, returned, old_rows)
    second_x = trade(second_ortho.reshape(4, out_block, width), ("h", "m"))
    if quarter > 1:
        second_x = lax.ppermute(second_x, ("i", "b"), fold_pairs(quarter))


    head_count = gate_head.shape[0]
    small = sum_flips(tie(small, second_ortho), (("c",),))
    grad_gate = small[:head_count]
    grad_norm = small[head_count : head_count + 2]
    grad_head = small[head_count + 2, : 2 * head_dim].reshape(2, head_dim)
    new_mom_norm = 0.5 * mom_norm + 0.5 * grad_norm
    new_mom_head = 0.5 * mom_head + 0.5 * grad_head
    new_mom_gate = 0.5 * mom_gate_head + 0.5 * grad_gate
    new_norm = norm_gains - VECTOR_RATE * new_mom_norm
    new_head = head_gains - VECTOR_RATE * new_mom_head
    new_gate = gate_head.astype(F32) - VECTOR_RATE * new_mom_gate

    seq_len = tok_dev * n * 4
    out_boost = math.sqrt(width / max(1, 16384 // seq_len))
    rate = lambda rows: MATRIX_RATE * math.sqrt(rows * 8 * n)
    first_rates = {DOWN: rate(ff_block), GATE: rate(ff_block), UP: rate(ff_block)}
    second_rates = {
        QUERY: rate(out_block),
        OUT: out_boost * rate(out_block),
        KEY: rate(small_block),
        VALUE: rate(small_block),
    }
    q_at, k_at, v_at = 0, out_block, out_block + small_block
    o_at = v_at + small_block
    gate_at, up_at, down_at = (o_at + out_block + k * ff_block for k in range(3))
    g_gateup, g_down, m_gateup, m_down = settle(
        first_g, first_moms, first_moms, first_places, None
    )
    g_query, g_keyval, g_outproj, m_query, m_keyval, m_outproj = settle(
        second_g, second_moms, second_moms, second_places, None
    )
    n_gateup, n_down = settle(
        first_x,
        [old_rows],
        first_moms,
        (((GATE, gate_at), (UP, up_at)), ((DOWN, down_at),)),
        first_rates,
    )
    n_query, n_keyval, n_outproj = settle(
        second_x,
        [old_rows],
        second_moms,
        (((QUERY, q_at),), ((KEY, k_at), (VALUE, v_at)), ((OUT, o_at),)),
        second_rates,
    )

    return (
        output[None],
        grad_input[None],
        grad_norm,
        grad_head,
        grad_gate,
        g_query,
        g_keyval,
        g_outproj,
        g_gateup,
        g_down,
        new_mom_norm,
        new_mom_head,
        new_mom_gate,
        m_query,
        m_keyval,
        m_outproj,
        m_gateup,
        m_down,
        new_norm,
        new_head,
        new_gate,
        n_query,
        n_keyval,
        n_outproj,
        n_gateup,
        n_down,
    )


def solution(mesh):
    count = mesh.devices.size
    n = count // 8
    sizes = {"h": 2, "m": 2, "i": n // 4, "b": 2, "c": 2, "x": 2}
    fine = Mesh(mesh.devices.reshape(tuple(sizes[axis] for axis in ALL)), ALL)
    rows3 = P("x", CTX, None)
    own2 = P(ALL, None)
    own3 = P(None, ALL, None)
    half2 = P("x", None)
    half3 = P(None, "x", None)
    owners = (own2, own3, own2, own3, own2)
    return jax.shard_map(
        functools.partial(on_device, n),
        mesh=fine,
        in_specs=(rows3, rows3, P(), P(), P(), P(), half2, half3, half2, half3, half2)
        + (P(), P(), P())
        + owners,
        out_specs=(rows3, rows3, P(), P(), P())
        + owners
        + (P(), P(), P())
        + owners
        + (P(), P(), P())
        + owners,
        check_vma=False,
    )
```

```python
import functools
import math

import jax
import jax.numpy as jnp
from jax import lax
from jax.experimental import pallas as pl
from jax.experimental.pallas import tpu as pltpu
from jax.sharding import Mesh, PartitionSpec as P

NS_STEPS = 5
NORM_EPS = 1e-06
ROPE_BASE = 1000000.0
NS_A = 3.4445
NS_B = -4.775
NS_C = 2.0315
MATRIX_RATE = 0.03
VECTOR_RATE = 0.003
CTX = ("h", "m", "i", "b", "c")
ALL = CTX + ("x",)
F32 = jnp.float32
BF16 = jnp.bfloat16


def nt(p, q):
    return lax.dot_general(p, q, (((1,), (1,)), ((), ())), preferred_element_type=F32)


def nn(p, q):
    return lax.dot_general(p, q, (((1,), (0,)), ((), ())), preferred_element_type=F32)


def tn(p, q):
    return lax.dot_general(p, q, (((0,), (0,)), ((), ())), preferred_element_type=F32)


def flip(v, *axes):
    last = 2 ** len(axes) - 1
    return lax.ppermute(v, tuple(sorted(axes, key=ALL.index)), [(j, j ^ last) for j in range(last + 1)])


NEAR = (("x",), ("b",), ("b", "x"))


def gather_near(v):
    return [v] + [flip(v, *axes) for axes in NEAR]


def pieces_far(near):
    return near + [flip(member, "c") for member in near]


def join_kernel(*refs):
    ins, out, sems = refs[:-2], refs[-2], refs[-1]
    rows = ins[0].shape[0]
    run_copies([(ref, out.at[pl.ds(k * rows, rows)]) for k, ref in enumerate(ins)], sems)


def join(pieces):
    rows, width = pieces[0].shape
    count = len(pieces)
    return pl.pallas_call(
        join_kernel,
        out_shape=jax.ShapeDtypeStruct((count * rows, width), pieces[0].dtype),
        in_specs=[HBM_SPEC] * count,
        out_specs=VMEM_SPEC,
        scratch_shapes=[pltpu.SemaphoreType.DMA((count,))],
        compiler_params=SMALL,
        cost_estimate=pl.CostEstimate(
            flops=0, bytes_accessed=4 * count * rows * width, transcendentals=0
        ),
        name="join",
    )(*pieces)


def gather_far(near):
    return join(pieces_far(near))


def gather_group(v):
    return gather_far(gather_near(v))


def sum_core(part):
    half = part.shape[0] // 2
    return part[:half] + flip(part[half:].astype(BF16), "c").astype(F32)


def sum_near(part):
    rows = part.shape[0] // 4
    low = part.astype(BF16)
    total = part[:rows]
    for slot, axes in enumerate(NEAR, 1):
        total = total + flip(low[slot * rows : (slot + 1) * rows], *axes).astype(F32)
    return total


def sum_group(part):
    return sum_near(sum_core(part))


def sum_flips(v, flips):
    return sum((flip(v, *axes) for axes in flips), v)


def swap_halves(v, my_half, my_x):
    other = lax.ppermute(v, ("h", "x"), [(1, 2), (2, 1)])
    return jnp.where(my_half == my_x, v, other)


DOWN, NONE, GATE, UP = range(4)
QUERY, OUT, KEY, VALUE = range(4)

def trade(v, axes):
    return lax.all_to_all(v, axes, split_axis=0, concat_axis=0, tiled=True)


def turned(v):
    return jnp.stack([v[0], v[2], v[1], v[3]])


def fold_pairs(q):
    return [(i * 2 + b, b * q + i) for i in range(q) for b in range(2)]


VMEM_SPEC = pl.BlockSpec(memory_space=pltpu.VMEM)
SMEM_SPEC = pl.BlockSpec(memory_space=pltpu.SMEM)
SMALL = pltpu.CompilerParams(vmem_limit_bytes=32 * 2**20)
LARGE = pltpu.CompilerParams(vmem_limit_bytes=60 * 2**20)


HBM_SPEC = pl.BlockSpec(memory_space=pl.ANY)
FAR_SPEC = pl.BlockSpec(memory_space=pltpu.HBM)


def run_copies(pairs, sems):
    copies = [pltpu.make_async_copy(p, q, sems.at[k]) for k, (p, q) in enumerate(pairs)]
    for copy in copies:
        copy.start()
    for copy in copies:
        copy.wait()


def slices_kernel(sub_ref, wq, wkv, wo, wgu, wd, gate, w_in, o_out, gu_out, d_out, sems):
    sub = sub_ref[0, 0]
    q_rows, kv_rows = o_out.shape[0], wkv.shape[1] // 4

    def part(ref, rows):
        return ref.at[pl.ds(pl.multiple_of(sub * rows, rows), rows)]

    pairs = [
        (part(wq, q_rows), w_in.at[pl.ds(0, q_rows)]),
        (part(wkv.at[0], kv_rows), w_in.at[pl.ds(q_rows, kv_rows)]),
        (part(wkv.at[1], kv_rows), w_in.at[pl.ds(q_rows + kv_rows, kv_rows)]),
        (gate, w_in.at[pl.ds(q_rows + 2 * kv_rows, gate.shape[0])]),
        (part(wo, q_rows), o_out),
    ]
    pairs += [(part(wgu.at[g], d_out.shape[0]), gu_out.at[g]) for g in range(2)]
    pairs.append((part(wd, d_out.shape[0]), d_out))
    run_copies(pairs, sems)


def weight_slices(sub, w_query, w_keyval, w_outproj, w_gateup, w_down, gate):
    width = w_query.shape[1]
    q_rows, kv_rows = w_query.shape[0] // 4, w_keyval.shape[1] // 4
    ff_rows = w_down.shape[0] // 4
    w_in, wo, wgu, wd = pl.pallas_call(
        slices_kernel,
        out_shape=[
            jax.ShapeDtypeStruct((q_rows + 2 * kv_rows + gate.shape[0], width), BF16),
            jax.ShapeDtypeStruct((q_rows, width), BF16),
            jax.ShapeDtypeStruct((2, ff_rows, width), BF16),
            jax.ShapeDtypeStruct((ff_rows, width), BF16),
        ],
        in_specs=[SMEM_SPEC] + [FAR_SPEC] * 5 + [HBM_SPEC],
        out_specs=[VMEM_SPEC] * 4,
        scratch_shapes=[pltpu.SemaphoreType.DMA((8,))],
        compiler_params=LARGE,
        cost_estimate=pl.CostEstimate(flops=0, bytes_accessed=2**23, transcendentals=0),
        name="slices",
    )(
        sub.reshape(1, 1),
        w_query,
        w_keyval,
        w_outproj,
        w_gateup,
        w_down,
        gate,
    )
    return w_in, wo, wgu.reshape(2 * ff_rows, width), wd


def owned_kernel(spot_ref, *refs):
    ins, outs, sems = refs[:5], refs[-3:-1], refs[-1]
    pairs = []
    for k, out in enumerate(outs):
        spot, at = spot_ref[0, k], 0
        for ref in ins:
            rows = ref.shape[-2] // row_blocks(out, ins)
            span = pl.ds(pl.multiple_of(spot * rows, rows), rows)
            for part in [ref.at[j] for j in range(2)] if len(ref.shape) == 3 else [ref]:
                pairs.append((part.at[span], out.at[pl.ds(at, rows)]))
                at += rows
    run_copies(pairs, sems)


def row_blocks(out, ins):
    total = sum(ref.shape[-2] * (2 if len(ref.shape) == 3 else 1) for ref in ins)
    return total // out.shape[0]


def owned_rows(spots, weights, n, *tokens):
    rows = sum(w.shape[-2] * (2 if w.ndim == 3 else 1) for w in weights) // (4 * n)
    out = jax.ShapeDtypeStruct((rows, weights[0].shape[-1]), BF16)
    return pl.pallas_call(
        owned_kernel,
        out_shape=[out, out],
        in_specs=[SMEM_SPEC] + [FAR_SPEC] * 5 + [HBM_SPEC] * len(tokens),
        out_specs=[VMEM_SPEC] * 2,
        scratch_shapes=[pltpu.SemaphoreType.DMA((14,))],
        compiler_params=LARGE,
        cost_estimate=pl.CostEstimate(flops=0, bytes_accessed=2**22, transcendentals=0),
        name="owned",
    )(spots, *weights, *tokens)


def tie(value, *tokens):
    return pl.pallas_call(
        lambda *refs: None,
        out_shape=jax.ShapeDtypeStruct(value.shape, value.dtype),
        in_specs=[HBM_SPEC] * (1 + len(tokens)),
        out_specs=HBM_SPEC,
        input_output_aliases={0: 0},
        cost_estimate=pl.CostEstimate(flops=0, bytes_accessed=0, transcendentals=0),
        name="tie",
    )(value, *tokens)


def pack_kernel(places, ins, *refs):
    out = refs[-1]
    out[...] = jnp.zeros_like(out)
    for ref, item in zip(refs[:ins], places):
        rows = ref.shape[-2]
        for j, (member, first) in enumerate(item):
            source = ref[j] if len(ref.shape) == 3 else ref[...]
            out[member, first : first + rows] = source.astype(BF16)


def pack(arrays, places, height, *tokens):
    width = arrays[0].shape[-1]
    return pl.pallas_call(
        functools.partial(pack_kernel, places, len(arrays)),
        out_shape=jax.ShapeDtypeStruct((4, height, width), BF16),
        in_specs=[VMEM_SPEC] * len(arrays) + [HBM_SPEC] * len(tokens),
        out_specs=VMEM_SPEC,
        compiler_params=SMALL,
        cost_estimate=pl.CostEstimate(flops=0, bytes_accessed=24 * height * width, transcendentals=0),
        name="pack",
    )(*arrays, *tokens)


def held_kernel(v_ref, *refs):
    refs[-1][...] = v_ref[...]


def held(v, *tokens):
    return pl.pallas_call(
        held_kernel,
        out_shape=jax.ShapeDtypeStruct(v.shape, v.dtype),
        in_specs=[VMEM_SPEC] + [HBM_SPEC] * len(tokens),
        out_specs=VMEM_SPEC,
        compiler_params=SMALL,
        cost_estimate=pl.CostEstimate(flops=0, bytes_accessed=4 * v.size, transcendentals=0),
        name="held",
    )(v, *tokens)


def settle_kernel(places, rates, items, *refs):
    if rates is None:
        count = len(places)
        olds, outs = refs[:count], refs[count:]
    else:
        old_ref, outs = refs[0], refs[1:]
    for a, item in enumerate(places):
        rows = outs[a].shape[-2]
        for j, place in enumerate(item):
            at = (j,) if len(outs[a].shape) == 3 else (slice(None),)
            member, first = place if rates is not None else (place, 0)
            value = items[member, :rows].astype(F32)
            if rates is None:
                outs[a][at] = value
                outs[count + a][at] = 0.5 * olds[a][at] + 0.5 * value
            else:
                old = old_ref[first : first + rows, :].astype(F32)
                outs[a][at] = old - rates[member] * value


def settle(items, olds, shapes, places, rates):
    shapes = [jax.ShapeDtypeStruct(v.shape, F32) for v in shapes]
    shapes = shapes * (2 if rates is None else 1)
    return pl.pallas_call(
        functools.partial(settle_kernel, places, rates),
        out_shape=shapes,
        in_specs=[VMEM_SPEC] * (1 + len(olds)),
        out_specs=[VMEM_SPEC] * len(shapes),
        compiler_params=SMALL,
        cost_estimate=pl.CostEstimate(flops=0, bytes_accessed=12 * items.size, transcendentals=0),
        name="settle",
    )(items, *olds)


TILE = 512
ATTENTION = pltpu.CompilerParams(vmem_limit_bytes=44 * 2**20)


def tile_at(j, size=TILE, offset=0):
    return pl.ds(pl.multiple_of(j * size + offset, size), size)


def shape_of(dtype, *shape):
    return jax.ShapeDtypeStruct(shape, dtype)


def cost(microseconds):
    return pl.CostEstimate(
        flops=int(microseconds * 1.15e9), bytes_accessed=2**20, transcendentals=0
    )


def head_scale(raw):
    return lax.rsqrt(jnp.mean(raw * raw, axis=-1, keepdims=True) + NORM_EPS)


def head_back(grad, raw, cosine, sine, gain):
    grad = grad * cosine - pltpu.roll(grad, grad.shape[1] // 2, 1) * sine
    scale = head_scale(raw)
    unit = raw * scale
    pushed = grad * gain
    back = scale * (pushed - unit * jnp.mean(pushed * unit, axis=-1, keepdims=True))
    return back, jnp.sum(grad * unit, axis=0, keepdims=True)


def project_kernel(heads, n_ref, w_ref, cos_ref, sin_ref, gain_ref, q_ref, kv_ref, lg_ref, raw_ref):
    rows, dim = n_ref.shape[0], cos_ref.shape[1]

    @pl.loop(0, rows // 256)
    def _(t):
        span = tile_at(t, 256)
        out = nt(n_ref[span, :], w_ref[...])
        cosine, sine = cos_ref[span, :], sin_ref[span, :]
        for j in range(heads + 1):
            raw = out[:, j * dim : (j + 1) * dim]
            raw_ref[j, span, :] = raw
            which = slice(0, 1) if j < heads else slice(1, 2)
            unit = raw * head_scale(raw) * gain_ref[which, :]
            turned_rows = unit * cosine + pltpu.roll(unit, dim // 2, 1) * sine
            if j < heads:
                q_ref[j, span, :] = turned_rows.astype(BF16)
            else:
                kv_ref[0, span, :] = turned_rows.astype(BF16)
        kv_ref[1, span, :] = out[:, (heads + 1) * dim : (heads + 2) * dim].astype(BF16)
        lg_ref[span, :] = jax.nn.sigmoid(out[:, (heads + 2) * dim : (heads + 3) * dim])


def project(normed, w_in, cosine, sine, gains):
    rows, dim = cosine.shape
    heads = w_in.shape[0] // dim - 3
    return pl.pallas_call(
        functools.partial(project_kernel, heads),
        out_shape=[
            shape_of(BF16, heads, rows, dim),
            shape_of(BF16, 2, rows, dim),
            shape_of(F32, rows, dim),
            shape_of(F32, heads + 1, rows, dim),
        ],
        in_specs=[VMEM_SPEC] * 5,
        out_specs=[VMEM_SPEC] * 4,
        compiler_params=ATTENTION,
        cost_estimate=cost(6),
        name="project",
    )(normed, w_in, cosine, sine, gains)


def widened(values):
    return jnp.concatenate([values, jnp.ones_like(values)], axis=1)


def attend_kernel(scale, q_ref, lg_ref, qp_ref, kp_ref, *refs):
    pieces, (att_ref, tot_ref, gated_ref) = refs[:-3], refs[-3:]
    heads, rows, dim = q_ref.shape
    for h in range(heads):

        @pl.loop(0, rows // TILE)
        def _(i):
            span = tile_at(i)
            query, place = q_ref[h, span, :], qp_ref[span, :]
            total = jnp.zeros((TILE, 2 * dim), F32)
            for number, kv_ref in enumerate(pieces):
                offset = number * kv_ref.shape[1]

                def step(j, acc, kv_ref=kv_ref, offset=offset):
                    scores = nt(query, kv_ref[0, tile_at(j), :])
                    seen = kp_ref[:, tile_at(j, offset=offset)] <= place
                    weights = jnp.where(seen, jnp.exp2(scores * scale), 0.0)
                    return acc + nn(weights.astype(BF16), widened(kv_ref[1, tile_at(j), :]))

                total = lax.fori_loop(0, kv_ref.shape[1] // TILE, step, total)
            weight = total[:, dim : dim + 1]
            attended = total[:, :dim] / weight
            att_ref[h, span, :] = attended
            tot_ref[h, span, :] = weight
            gated_ref[span, h * dim : (h + 1) * dim] = (
                attended * lg_ref[span, h : h + 1]
            ).astype(BF16)


def attend(query, sigmoids, pieces, q_place, k_place, scale, *tokens):
    heads, rows, dim = query.shape
    count = len(pieces)
    kernel = functools.partial(attend_kernel, scale * math.log2(math.e))

    def without_tokens(*refs):
        kernel(*refs[: 4 + count], *refs[4 + count + len(tokens) :])

    return pl.pallas_call(
        without_tokens,
        out_shape=[
            shape_of(F32, heads, rows, dim),
            shape_of(F32, heads, rows, 1),
            shape_of(BF16, rows, heads * dim),
        ],
        in_specs=[VMEM_SPEC] * (4 + count) + [HBM_SPEC] * len(tokens),
        out_specs=[VMEM_SPEC] * 3,
        compiler_params=ATTENTION,
        cost_estimate=cost(12),
        name="attend",
    )(query, sigmoids, q_place[:, None], k_place[None, :], *pieces, *tokens)


def before_kernel(b_ref, w_ref, att_ref, tot_ref, lg_ref, bw_ref, dl_ref):
    heads, rows, dim = att_ref.shape
    lanes = lax.broadcasted_iota(jnp.int32, (256, dim), 1)

    @pl.loop(0, rows // 256)
    def _(t):
        span = tile_at(t, 256)
        grad = nt(b_ref[span, :], w_ref[...])
        logits = jnp.zeros((256, dim), F32)
        for h in range(heads):
            part = grad[:, h * dim : (h + 1) * dim]
            sig = lg_ref[span, h : h + 1]
            total = tot_ref[h, span, :]
            along = jnp.sum(part * att_ref[h, span, :], axis=-1, keepdims=True)
            logits = jnp.where(lanes == h, sig * (1.0 - sig) * along, logits)
            bw_ref[h, span, :dim] = (part * (sig / total)).astype(BF16)
            corr = -sig * along / total
            high = corr.astype(BF16).astype(F32)
            extra = jnp.where(lanes == 0, high, jnp.where(lanes == 1, corr - high, 0.0))
            bw_ref[h, span, dim:] = extra.astype(BF16)
        dl_ref[span, :] = logits.astype(BF16)


def before_attention(dbranch, wo, attended, total, sigmoids):
    heads, rows, dim = attended.shape
    return pl.pallas_call(
        before_kernel,
        out_shape=[shape_of(BF16, heads, rows, 2 * dim), shape_of(BF16, rows, dim)],
        in_specs=[VMEM_SPEC] * 5,
        out_specs=[VMEM_SPEC] * 2,
        compiler_params=ATTENTION,
        cost_estimate=cost(5),
        name="before",
    )(dbranch, wo, attended, total, sigmoids)


def attend_back_kernel(
    scale, count, q_ref, bw_ref, raw_ref, cos_ref, sin_ref, gain_ref, qp_ref, kp_ref, *refs
):
    pieces = refs[:count]
    dq_ref, terms_ref = refs[count : count + 2]
    outs, sums = refs[count + 2 : 2 * count + 2], refs[2 * count + 2 :]
    heads, rows, dim = q_ref.shape
    grow = scale * math.log2(math.e)
    for ref in sums:
        ref[...] = jnp.zeros_like(ref)
    terms_ref[...] = jnp.zeros_like(terms_ref)
    for h in range(heads):

        @pl.loop(0, rows // TILE)
        def _(i):
            span = tile_at(i)
            query, back, place = q_ref[h, span, :], bw_ref[h, span, :], qp_ref[:, span]
            total = jnp.zeros((TILE, dim), F32)
            for number, (kv_ref, sum_ref) in enumerate(zip(pieces, sums)):
                offset = number * kv_ref.shape[1]

                def step(j, acc, kv_ref=kv_ref, sum_ref=sum_ref, offset=offset):
                    keys = tile_at(j)
                    key = kv_ref[0, keys, :]
                    seen = kp_ref[tile_at(j, offset=offset), :] <= place
                    weights = jnp.where(seen, jnp.exp2(nt(key, query) * grow), 0.0)
                    push = nt(widened(kv_ref[1, keys, :]), back)
                    dscore = (weights * push * scale).astype(BF16)
                    sum_ref[1, keys, :] += nn(weights.astype(BF16), back[:, :dim])
                    sum_ref[0, keys, :] += nn(dscore, query)
                    return acc + tn(dscore, key)

                total = lax.fori_loop(0, kv_ref.shape[1] // TILE, step, total)
            grad, terms = head_back(
                total, raw_ref[h, span, :], cos_ref[span, :], sin_ref[span, :], gain_ref[0:1, :]
            )
            dq_ref[span, h * dim : (h + 1) * dim] = grad.astype(BF16)
            terms_ref[...] += terms

    for out, ref in zip(outs, sums):
        out[...] = ref[...].astype(out.dtype)


def attend_back(query, back, raw, cosine, sine, gains, pieces, q_place, k_place, scale):
    heads, rows, dim = query.shape
    count = len(pieces)
    return pl.pallas_call(
        functools.partial(attend_back_kernel, scale, count),
        out_shape=[shape_of(BF16, rows, heads * dim), shape_of(F32, 1, dim)]
        + [shape_of(BF16 if k else F32, *piece.shape) for k, piece in enumerate(pieces)],
        in_specs=[VMEM_SPEC] * (8 + count),
        out_specs=[VMEM_SPEC] * (2 + count),
        scratch_shapes=[pltpu.VMEM(piece.shape, F32) for piece in pieces],
        compiler_params=ATTENTION,
        cost_estimate=cost(18),
        name="attend_back",
    )(
        query, back, raw, cosine, sine, gains, q_place[None, :], k_place[:, None], *pieces
    )


def keys_kernel(own_ref, far_ref, raw_ref, cos_ref, sin_ref, gain_ref, dl_ref, out_ref, terms_ref):
    rows, dim = cos_ref.shape
    terms_ref[...] = jnp.zeros_like(terms_ref)

    @pl.loop(0, rows // 256)
    def _(t):
        span = tile_at(t, 256)
        both = [own_ref[k, span, :] + far_ref[k, span, :].astype(F32) for k in range(2)]
        grad, terms = head_back(
            both[0], raw_ref[raw_ref.shape[0] - 1, span, :], cos_ref[span, :], sin_ref[span, :], gain_ref[1:2, :]
        )
        terms_ref[...] += terms
        out_ref[span, :dim] = grad.astype(BF16)
        out_ref[span, dim : 2 * dim] = both[1].astype(BF16)
        out_ref[span, 2 * dim :] = dl_ref[span, :]


def keys_back(own, far, raw, cosine, sine, gains, dlogit):
    rows, dim = cosine.shape
    return pl.pallas_call(
        keys_kernel,
        out_shape=[shape_of(BF16, rows, 3 * dim), shape_of(F32, 1, dim)],
        in_specs=[VMEM_SPEC] * 7,
        out_specs=[VMEM_SPEC] * 2,
        compiler_params=ATTENTION,
        cost_estimate=cost(3),
        name="keys",
    )(own, far, raw, cosine, sine, gains, dlogit)


def rms_scale(v):
    return lax.rsqrt(jnp.mean(v * v, axis=-1, keepdims=True) + NORM_EPS)


def norm_back(grad, scaled, rscale, gains):
    pushed = grad * gains
    return rscale * (pushed - scaled * jnp.mean(pushed * scaled, axis=-1, keepdims=True))


def mirror(ref, tile):
    for j in range(ref.shape[0] // tile):
        for i in range(j):
            block = ref[i * tile : (i + 1) * tile, j * tile : (j + 1) * tile].astype(F32)
            ref[j * tile : (j + 1) * tile, i * tile : (i + 1) * tile] = block.T.astype(BF16)


def schulz_kernel(count, start_ref, *refs):
    pieces = refs[:count]
    o_ref, x_ref, x_own, e_gram, e_poly, e_half, gram, poly, half, sems = refs[-10:]
    piece = pieces[0].shape[0]
    copies = [
        pltpu.make_async_copy(ref, x_ref.at[pl.ds(k * piece, piece)], sems.at[k])
        for k, ref in enumerate(pieces)
    ]
    for copy in copies:
        copy.start()
    for copy in copies:
        copy.wait()
    chunk = min(1024, x_ref.shape[0])
    width = x_ref.shape[1]
    own = o_ref.shape[0]
    tile = 256
    blocks = [(slice(0, (j + 1) * tile), slice(j * tile, (j + 1) * tile)) for j in range(width // tile)]
    diag = (
        lax.broadcasted_iota(jnp.int32, (tile, tile), 0)
        == lax.broadcasted_iota(jnp.int32, (tile, tile), 1)
    ).astype(F32)

    def trace(ref):
        total = jnp.zeros((tile, tile), F32)
        for _, cols in blocks:
            total = total + ref[cols, cols] * diag
        return jnp.sum(jnp.sum(total, axis=1, keepdims=True), axis=0, keepdims=True)

    def settle_gram(scale, centre):
        for rows, cols in blocks:
            part = e_gram[rows, cols]
            e_gram[rows, cols] = part if scale is None else part * scale
            e_gram[cols, cols] -= centre * diag
            gram[rows, cols] = e_gram[rows, cols].astype(BF16)
        mirror(gram, tile)

    def make_poly(d):
        p = NS_A + NS_B * d + NS_C * d * d
        for rows, cols in blocks:
            part = (NS_B + 2.0 * NS_C * d) * e_gram[rows, cols] + NS_C * nn(
                gram[rows, :], gram[:, cols]
            )
            e_poly[rows, cols] = part
            poly[rows, cols] = part.astype(BF16)
        mirror(poly, tile)
        return p

    def advance(d, p):
        for rows, cols in blocks:
            part = d * e_poly[rows, cols] + p * e_gram[rows, cols] + nn(gram[rows, :], poly[:, cols])
            e_half[rows, cols] = part
            half[rows, cols] = part.astype(BF16)
        mirror(half, tile)
        q = d * p
        for rows, cols in blocks:
            e_gram[rows, cols] = (
                q * e_poly[rows, cols] + p * e_half[rows, cols] + nn(half[rows, :], poly[:, cols])
            )
        centre = trace(e_gram) * (1.0 / width)
        settle_gram(None, centre)
        return q * p + centre

    def apply(p):
        now = x_own[...]
        return p * now + nn(now.astype(BF16), poly[...])

    for rows, cols in blocks:
        e_gram[rows, cols] = lax.fori_loop(
            0,
            x_ref.shape[0] // chunk,
            lambda r, acc: acc
            + tn(
                x_ref[pl.ds(pl.multiple_of(r * chunk, chunk), chunk), rows],
                x_ref[pl.ds(pl.multiple_of(r * chunk, chunk), chunk), cols],
            ),
            jnp.zeros((rows.stop, tile), F32),
        )
    square = trace(e_gram)
    inv = 1.0 / (jnp.sqrt(square) + 1e-07)
    first = square * inv * inv * (1.0 / width)
    settle_gram(inv * inv, first)
    x_own[...] = x_ref[pl.ds(pl.multiple_of(start_ref[0, 0], own), own), :].astype(F32) * inv

    def sweep(_, d):
        p = make_poly(d)
        x_own[...] = apply(p)
        return advance(d, p)

    d = lax.fori_loop(0, NS_STEPS - 1, sweep, first)
    o_ref[...] = apply(make_poly(d)).astype(BF16)


def orthogonal(pieces, firsts, own, *tokens):
    count = len(pieces)
    rows, width = count * pieces[0].shape[0], pieces[0].shape[1]
    wide = pltpu.VMEM((width, width), F32)
    low = pltpu.VMEM((width, width), BF16)
    return pl.pallas_call(
        functools.partial(schulz_kernel, count),
        out_shape=jax.ShapeDtypeStruct((own, width), BF16),
        in_specs=[SMEM_SPEC] + [HBM_SPEC] * (count + len(tokens)),
        out_specs=VMEM_SPEC,
        scratch_shapes=[
            pltpu.VMEM((rows, width), BF16),
            pltpu.VMEM((own, width), F32),
            wide,
            wide,
            wide,
            low,
            low,
            low,
            pltpu.SemaphoreType.DMA((count,)),
        ],
        compiler_params=pltpu.CompilerParams(vmem_limit_bytes=48 * 2**20),
        cost_estimate=pl.CostEstimate(
            flops=44 * 2**30, bytes_accessed=4 * rows * width, transcendentals=0
        ),
        name="schulz",
    )(firsts, *pieces, *tokens)


def on_device(
    n,
    tokens,
    cotangent,
    pair_order,
    norm_gains,
    head_gains,
    gate_head,
    w_query,
    w_keyval,
    w_outproj,
    w_gateup,
    w_down,
    mom_norm,
    mom_head,
    mom_gate_head,
    mom_query,
    mom_keyval,
    mom_outproj,
    mom_gateup,
    mom_down,
):
    quarter = n // 4
    my_h, my_m, my_i = lax.axis_index("h"), lax.axis_index("m"), lax.axis_index("i")
    my_b, my_c, my_x = lax.axis_index("b"), lax.axis_index("c"), lax.axis_index("x")
    me = lax.axis_index(ALL)
    everywhere = ("h", "m", "i")
    sub = my_c * 2 + my_b
    my_plane = my_h * 2 + my_m
    tok_dev, width = tokens.shape[1], tokens.shape[2]
    head_dim = head_gains.shape[1]
    scale = 1.0 / math.sqrt(head_dim)
    piece = tok_dev // 2
    group_rows = 8 * tok_dev

    rows_tok = swap_halves(tokens[0], my_h, my_x)
    xf = rows_tok.astype(F32)
    r1 = rms_scale(xf)
    y1 = xf * r1
    normed_rows = (y1 * norm_gains[0]).astype(BF16)
    q_rows = w_query.shape[0] // 4
    kv_rows = w_keyval.shape[1] // 4
    heads_here = q_rows // head_dim
    wgate = lax.dynamic_slice_in_dim(gate_head, (my_x * 4 + sub) * heads_here, heads_here, 0)
    gate_pad = 128 - heads_here
    small_block = w_keyval.shape[1] // (4 * n)
    out_block = w_outproj.shape[0] // (4 * n)
    ff_block = w_gateup.shape[1] // (4 * n)
    ff_rows = n * ff_block
    w_in, wo, wgu, wd = weight_slices(
        sub,
        w_query,
        w_keyval,
        w_outproj,
        w_gateup,
        w_down,
        jnp.pad(wgate, ((0, gate_pad), (0, 0))),
    )


    order_ids = jnp.arange(pair_order.shape[0], dtype=jnp.int32)

    def group_place(r_index):
        flips = jnp.arange(8, dtype=jnp.int32)
        dev_x = my_x ^ (flips & 1)
        dev_b = my_b ^ ((flips >> 1) & 1)
        dev_c = my_c ^ (flips >> 2)
        ctx_ids = ((dev_x * (n // 2) + r_index) * 2 + dev_b) * 2 + dev_c
        owner = jnp.sum(
            jnp.where(ctx_ids[:, None] == order_ids[None, :], pair_order[None, :], 0), axis=1
        )
        blocks = jnp.stack([owner, 2 * pair_order.shape[0] - 1 - owner], axis=1)
        spots = blocks[:, :, None] * piece + jnp.arange(piece, dtype=jnp.int32)
        return spots.reshape(group_rows)

    my_r = my_m * quarter + my_i
    place = group_place(my_r)
    if n == 4:
        key_place = jnp.concatenate([place, group_place(my_r ^ 1)])
    else:
        key_place = jnp.concatenate([group_place(r) for r in range(n // 2)])

    def key_pieces(kv):
        if n == 4:
            return [kv, flip(kv, "m")]
        return [lax.all_gather(kv, ("m", "i"), axis=1, tiled=True)]

    def key_sums(parts):
        if n == 4:
            return parts[0], flip(parts[1], "m")
        mine = lax.psum_scatter(parts[0], ("m", "i"), scatter_dimension=1, tiled=True)
        return mine, jnp.zeros(mine.shape, BF16)

    half = head_dim // 2
    inverse = ROPE_BASE ** (-(2.0 * jnp.arange(half, dtype=F32)) / head_dim)
    angles = place.astype(F32)[:, None] * inverse[None, :]
    cosine, sine = jnp.cos(angles), jnp.sin(angles)
    cosine = jnp.concatenate([cosine, cosine], axis=1)
    sine = jnp.concatenate([-sine, sine], axis=1)
    normed_rows = tie(normed_rows, w_in, cosine, sine, key_place)
    normed = gather_group(normed_rows)
    query_rows, kv_rows_here, sigmoids, raw = project(normed, w_in, cosine, sine, head_gains)
    rows_cot = swap_halves(held(cotangent[0], w_in, cosine), my_h, my_x)
    kv_all = key_pieces(kv_rows_here)
    cot_near = gather_near(tie(rows_cot, query_rows))
    attended, total, gated = attend(
        query_rows, sigmoids, kv_all, place, key_place, scale, rows_cot
    )
    gated = tie(gated, *cot_near)

    first_moms = (mom_gateup, mom_down)
    first_places = ((GATE, UP), (DOWN,))
    second_moms = (mom_query, mom_keyval, mom_outproj)
    second_places = ((QUERY,), (KEY, VALUE), (OUT,))
    old_items = pack(
        first_moms + second_moms,
        [[(member, 0) for member in place] for place in first_places]
        + [[(member, ff_block) for member in place] for place in second_places],
        ff_block + out_block,
        query_rows,
    )
    if quarter > 1:
        old_items = lax.ppermute(old_items, ("i", "b"), [(d, p) for p, d in fold_pairs(quarter)])
    old_items = trade(old_items, ("h", "m"))

    middle = xf + sum_group(nn(gated, wo))
    grad_all = gather_far(cot_near)
    r2 = rms_scale(middle)
    y2 = middle * r2
    hidden_in = gather_group((y2 * norm_gains[1]).astype(BF16))
    gate_up = nt(hidden_in, wgu)
    gate_part, up_part = gate_up[:, :ff_rows], gate_up[:, ff_rows:]
    sg = jax.nn.sigmoid(gate_part)
    silu = gate_part * sg
    hidden = (silu * up_part).astype(BF16)

    dhidden = nt(grad_all, wd)
    dgu = jnp.concatenate(
        [
            (dhidden * up_part * sg * (1.0 + gate_part * (1.0 - sg))).astype(BF16),
            (dhidden * silu).astype(BF16),
        ],
        axis=1,
    )
    dgu = tie(dgu, old_items)
    grad_gu = tn(dgu, hidden_in).astype(BF16)
    grad_d = tn(hidden, grad_all).astype(BF16)
    ff_grad = lax.psum_scatter(
        jnp.concatenate([grad_d, jnp.zeros_like(grad_d), grad_gu], axis=0),
        ("h", "m", "i"),
        scatter_dimension=0,
        tiled=True,
    )
    dhn = sum_group(nn(dgu, wgu))
    gout = rows_cot.astype(F32)
    norm_terms_mid = jnp.sum(dhn * y2, axis=0)
    dmiddle = gout + norm_back(dhn, y2, r2, norm_gains[1])
    out_sum = sum_core(nn(hidden, wd))
    dbranch = gather_group(tie(dmiddle.astype(BF16), out_sum))

    back_w, dlogit = before_attention(dbranch, wo, attended, total, sigmoids)

    def over_i(v):
        return lax.psum_scatter(v, "i", scatter_dimension=0, tiled=True) if quarter > 1 else v

    def blend(old, grad):
        return (0.5 * old.astype(F32) + 0.5 * grad.astype(F32)).astype(BF16)

    def padded(v, rows, height):
        blocks = v.reshape(4, rows, width)
        return jnp.pad(blocks, ((0, 0), (0, height - rows), (0, 0)))

    everyone = ("i", "b", "c", "x")
    mine_at = lax.axis_index(everyone)

    grad_o = over_i(tn(gated, dbranch).astype(BF16))
    grad_o = grad_o.astype(F32) + lax.ppermute(grad_o, ("h", "m"), [(0, 1), (3, 2)]).astype(F32)
    first_grad = ff_grad.reshape(4, ff_block, width)
    out_sum = tie(out_sum, back_w)

    dq, query_terms, *kv_sums = attend_back(
        query_rows, back_w, raw, cosine, sine, head_gains, kv_all, place, key_place, scale
    )
    out_rows = middle + sum_near(out_sum)
    first_mid = turned(trade(tie(first_grad, dq), ("c", "x")))
    kv_sums[0] = tie(kv_sums[0], out_rows)
    first_old, second_old = old_items[:, :ff_block], old_items[:, ff_block:]
    first_block = blend(first_old, first_mid).reshape(4 * ff_block, width)
    kv_own, kv_far = key_sums(kv_sums)
    dkv, key_terms = keys_back(kv_own, kv_far, raw, cosine, sine, head_gains, dlogit)
    first_start = lax.all_gather(tie(first_block, dkv), everyone, axis=0, tiled=True)
    head_terms = jnp.concatenate([query_terms, key_terms], axis=0)
    grad_q, grad_kv = tn(dq, normed), tn(dkv, normed)
    query_part = grad_q.reshape(n, 2, small_block, width)
    second_part = jnp.concatenate(
        [
            jnp.transpose(query_part, (1, 0, 2, 3)).reshape(q_rows, width),
            grad_kv[: 2 * kv_rows],
        ],
        axis=0,
    ).astype(BF16)
    dn_core = sum_core(nn(dq, w_in[:q_rows]) + nn(dkv, w_in[q_rows:]))
    dnormed = sum_near(dn_core)
    norm_terms_in = jnp.sum(dnormed * y1, axis=0)
    grad_rows = dmiddle + norm_back(dnormed, y1, r1, norm_gains[0])
    if quarter > 1:
        second_part = second_part.reshape(4, quarter, -1, width)
        second_part = lax.psum_scatter(second_part, "i", scatter_dimension=1, tiled=True)
    second_part = second_part.reshape(4, 4 * small_block, width)
    chunks = [
        lax.dynamic_index_in_dim(second_part, my_plane ^ k, 0, keepdims=False) for k in range(4)
    ]
    mine = chunks[0].astype(F32)
    for k, axes in ((1, ("m",)), (2, ("h",)), (3, ("h", "m"))):
        mine = mine + flip(chunks[k], *axes).astype(F32)
    mine = tie(mine.astype(BF16), dn_core)
    mine_sum = mine
    grad_o = tie(grad_o, mine_sum)
    grad_o = grad_o + lax.ppermute(grad_o.astype(BF16), ("h", "m"), [(2, 1)]).astype(F32)
    pair = flip(mine, "m")
    mine, pair = (v.reshape(4, small_block, width) for v in (mine, pair))
    second_grad = jnp.concatenate(
        [mine, jnp.where(my_plane == QUERY, pair, jnp.zeros_like(pair))], axis=1
    )
    second_grad = jnp.where(
        my_plane == OUT, grad_o.astype(BF16).reshape(4, out_block, width), second_grad
    )
    second_mid = turned(trade(second_grad, ("c", "x")))
    second_block = blend(second_old, second_mid).reshape(4 * out_block, width)
    small_z = (
        jnp.concatenate(
            [
                lax.dynamic_update_slice_in_dim(
                    jnp.zeros((gate_head.shape[0], width), F32),
                    grad_kv[2 * kv_rows : 2 * kv_rows + heads_here],
                    (my_x * 4 + sub) * heads_here,
                    0,
                ),
                norm_terms_in[None],
                norm_terms_mid[None],
                jnp.pad(head_terms.reshape(1, 2 * head_dim), ((0, 0), (0, width - 2 * head_dim))),
            ],
            axis=0,
        )
    )
    small = sum_flips(small_z, (("m",), ("h",), ("h", "m")))
    if quarter > 1:
        small = lax.psum(small, "i")
    small = sum_flips(small, NEAR)
    second_block = tie(second_block, small)
    second_start = lax.all_gather(second_block, everyone, axis=0, tiled=True)
    spot = me % (4 * n)
    mine_now, other_now = owned_rows(
        jnp.stack([spot, spot ^ 1]).reshape(1, 2),
        (w_query, w_keyval, w_outproj, w_gateup, w_down),
        n,
        second_block,
    )
    first_g = trade(tie(first_mid, second_block), ("h", "m"))
    if quarter > 1:
        first_g = lax.ppermute(first_g, ("i", "b"), fold_pairs(quarter))
    first_ortho = orthogonal(
        [first_start], (mine_at * (4 * ff_block)).reshape(1, 1), 4 * ff_block, other_now
    )
    second_ortho = orthogonal([second_start], (mine_at * (4 * out_block)).reshape(1, 1), 4 * out_block, first_ortho)
    sent = lax.ppermute(tie(grad_rows.astype(BF16), other_now), ("h", "x"), [(1, 2), (2, 1)])
    grad_input = jnp.where(my_h == my_x, grad_rows, sent.astype(F32))
    returned = jnp.concatenate(
        [first_ortho.reshape(4, ff_block, width), tie(second_mid, first_ortho)], axis=1
    )
    returned = trade(tie(returned, first_g, sent), ("h", "m"))
    if quarter > 1:
        returned = lax.ppermute(returned, ("i", "b"), fold_pairs(quarter))
    first_x, second_g = returned[:, :ff_block], returned[:, ff_block:]
    old_rows = jnp.where(my_x == my_h, mine_now, flip(tie(other_now, first_ortho), "x"))
    output = swap_halves(tie(out_rows.astype(BF16), first_ortho), my_h, my_x)
    second_ortho = tie(second_ortho, returned, old_rows, output)
    second_x = trade(second_ortho.reshape(4, out_block, width), ("h", "m"))
    if quarter > 1:
        second_x = lax.ppermute(second_x, ("i", "b"), fold_pairs(quarter))


    head_count = gate_head.shape[0]
    small = sum_flips(tie(small, second_ortho), (("c",),))
    grad_gate = small[:head_count]
    grad_norm = small[head_count : head_count + 2]
    grad_head = small[head_count + 2, : 2 * head_dim].reshape(2, head_dim)
    new_mom_norm = 0.5 * mom_norm + 0.5 * grad_norm
    new_mom_head = 0.5 * mom_head + 0.5 * grad_head
    new_mom_gate = 0.5 * mom_gate_head + 0.5 * grad_gate
    new_norm = norm_gains - VECTOR_RATE * new_mom_norm
    new_head = head_gains - VECTOR_RATE * new_mom_head
    new_gate = gate_head.astype(F32) - VECTOR_RATE * new_mom_gate

    seq_len = tok_dev * n * 4
    out_boost = math.sqrt(width / max(1, 16384 // seq_len))
    rate = lambda rows: MATRIX_RATE * math.sqrt(rows * 8 * n)
    first_rates = {DOWN: rate(ff_block), GATE: rate(ff_block), UP: rate(ff_block)}
    second_rates = {
        QUERY: rate(out_block),
        OUT: out_boost * rate(out_block),
        KEY: rate(small_block),
        VALUE: rate(small_block),
    }
    q_at, k_at, v_at = 0, out_block, out_block + small_block
    o_at = v_at + small_block
    gate_at, up_at, down_at = (o_at + out_block + k * ff_block for k in range(3))
    g_gateup, g_down, m_gateup, m_down = settle(
        first_g, first_moms, first_moms, first_places, None
    )
    g_query, g_keyval, g_outproj, m_query, m_keyval, m_outproj = settle(
        second_g, second_moms, second_moms, second_places, None
    )
    n_gateup, n_down = settle(
        first_x,
        [old_rows],
        first_moms,
        (((GATE, gate_at), (UP, up_at)), ((DOWN, down_at),)),
        first_rates,
    )
    n_query, n_keyval, n_outproj = settle(
        second_x,
        [old_rows],
        second_moms,
        (((QUERY, q_at),), ((KEY, k_at), (VALUE, v_at)), ((OUT, o_at),)),
        second_rates,
    )

    return (
        output[None],
        grad_input[None],
        grad_norm,
        grad_head,
        grad_gate,
        g_query,
        g_keyval,
        g_outproj,
        g_gateup,
        g_down,
        new_mom_norm,
        new_mom_head,
        new_mom_gate,
        m_query,
        m_keyval,
        m_outproj,
        m_gateup,
        m_down,
        new_norm,
        new_head,
        new_gate,
        n_query,
        n_keyval,
        n_outproj,
        n_gateup,
        n_down,
    )


def solution(mesh):
    count = mesh.devices.size
    n = count // 8
    sizes = {"h": 2, "m": 2, "i": n // 4, "b": 2, "c": 2, "x": 2}
    fine = Mesh(mesh.devices.reshape(tuple(sizes[axis] for axis in ALL)), ALL)
    rows3 = P("x", CTX, None)
    own2 = P(ALL, None)
    own3 = P(None, ALL, None)
    half2 = P("x", None)
    half3 = P(None, "x", None)
    owners = (own2, own3, own2, own3, own2)
    return jax.shard_map(
        functools.partial(on_device, n),
        mesh=fine,
        in_specs=(rows3, rows3, P(), P(), P(), P(), half2, half3, half2, half3, half2)
        + (P(), P(), P())
        + owners,
        out_specs=(rows3, rows3, P(), P(), P())
        + owners
        + (P(), P(), P())
        + owners
        + (P(), P(), P())
        + owners,
        check_vma=False,
    )
```

```python
import functools
import math

import jax
import jax.numpy as jnp
from jax import lax
from jax.experimental import pallas as pl
from jax.experimental.pallas import tpu as pltpu
from jax.sharding import Mesh, PartitionSpec as P

NS_STEPS = 5
NORM_EPS = 1e-06
ROPE_BASE = 1000000.0
NS_A = 3.4445
NS_B = -4.775
NS_C = 2.0315
MATRIX_RATE = 0.03
VECTOR_RATE = 0.003
CTX = ("h", "m", "i", "b", "c")
ALL = CTX + ("x",)
F32 = jnp.float32
BF16 = jnp.bfloat16


def nt(p, q):
    return lax.dot_general(p, q, (((1,), (1,)), ((), ())), preferred_element_type=F32)


def nn(p, q):
    return lax.dot_general(p, q, (((1,), (0,)), ((), ())), preferred_element_type=F32)


def tn(p, q):
    return lax.dot_general(p, q, (((0,), (0,)), ((), ())), preferred_element_type=F32)


def flip(v, *axes):
    last = 2 ** len(axes) - 1
    return lax.ppermute(v, tuple(sorted(axes, key=ALL.index)), [(j, j ^ last) for j in range(last + 1)])


NEAR = (("x",), ("b",), ("b", "x"))


def gather_near(v):
    return [v] + [flip(v, *axes) for axes in NEAR]


def pieces_far(near):
    return near + [flip(member, "c") for member in near]


def join_kernel(*refs):
    ins, out, sems = refs[:-2], refs[-2], refs[-1]
    rows = ins[0].shape[0]
    run_copies([(ref, out.at[pl.ds(k * rows, rows)]) for k, ref in enumerate(ins)], sems)


def join(pieces):
    rows, width = pieces[0].shape
    count = len(pieces)
    return pl.pallas_call(
        join_kernel,
        out_shape=jax.ShapeDtypeStruct((count * rows, width), pieces[0].dtype),
        in_specs=[HBM_SPEC] * count,
        out_specs=VMEM_SPEC,
        scratch_shapes=[pltpu.SemaphoreType.DMA((count,))],
        compiler_params=SMALL,
        cost_estimate=pl.CostEstimate(
            flops=0, bytes_accessed=4 * count * rows * width, transcendentals=0
        ),
        name="join",
    )(*pieces)


def gather_far(near):
    return join(pieces_far(near))


def gather_group(v):
    return gather_far(gather_near(v))


def sum_core(part):
    half = part.shape[0] // 2
    return part[:half] + flip(part[half:].astype(BF16), "c").astype(F32)


def sum_near(part):
    rows = part.shape[0] // 4
    low = part.astype(BF16)
    total = part[:rows]
    for slot, axes in enumerate(NEAR, 1):
        total = total + flip(low[slot * rows : (slot + 1) * rows], *axes).astype(F32)
    return total


def sum_group(part):
    return sum_near(sum_core(part))


def sum_flips(v, flips):
    return sum((flip(v, *axes) for axes in flips), v)


def swap_halves(v, my_half, my_x):
    other = lax.ppermute(v, ("h", "x"), [(1, 2), (2, 1)])
    return jnp.where(my_half == my_x, v, other)


DOWN, NONE, GATE, UP = range(4)
QUERY, OUT, KEY, VALUE = range(4)

def trade(v, axes):
    return lax.all_to_all(v, axes, split_axis=0, concat_axis=0, tiled=True)


def turned(v):
    return jnp.stack([v[0], v[2], v[1], v[3]])


def fold_pairs(q):
    return [(i * 2 + b, b * q + i) for i in range(q) for b in range(2)]


VMEM_SPEC = pl.BlockSpec(memory_space=pltpu.VMEM)
SMEM_SPEC = pl.BlockSpec(memory_space=pltpu.SMEM)
SMALL = pltpu.CompilerParams(vmem_limit_bytes=32 * 2**20)
LARGE = pltpu.CompilerParams(vmem_limit_bytes=60 * 2**20)


HBM_SPEC = pl.BlockSpec(memory_space=pl.ANY)
FAR_SPEC = pl.BlockSpec(memory_space=pltpu.HBM)


def run_copies(pairs, sems):
    copies = [pltpu.make_async_copy(p, q, sems.at[k]) for k, (p, q) in enumerate(pairs)]
    for copy in copies:
        copy.start()
    for copy in copies:
        copy.wait()


def slices_kernel(sub_ref, wq, wkv, wo, wgu, wd, gate, w_in, o_out, gu_out, d_out, sems):
    sub = sub_ref[0, 0]
    q_rows, kv_rows = o_out.shape[0], wkv.shape[1] // 4

    def part(ref, rows):
        return ref.at[pl.ds(pl.multiple_of(sub * rows, rows), rows)]

    pairs = [
        (part(wq, q_rows), w_in.at[pl.ds(0, q_rows)]),
        (part(wkv.at[0], kv_rows), w_in.at[pl.ds(q_rows, kv_rows)]),
        (part(wkv.at[1], kv_rows), w_in.at[pl.ds(q_rows + kv_rows, kv_rows)]),
        (gate, w_in.at[pl.ds(q_rows + 2 * kv_rows, gate.shape[0])]),
        (part(wo, q_rows), o_out),
    ]
    pairs += [(part(wgu.at[g], d_out.shape[0]), gu_out.at[g]) for g in range(2)]
    pairs.append((part(wd, d_out.shape[0]), d_out))
    run_copies(pairs, sems)


def weight_slices(sub, w_query, w_keyval, w_outproj, w_gateup, w_down, gate):
    width = w_query.shape[1]
    q_rows, kv_rows = w_query.shape[0] // 4, w_keyval.shape[1] // 4
    ff_rows = w_down.shape[0] // 4
    w_in, wo, wgu, wd = pl.pallas_call(
        slices_kernel,
        out_shape=[
            jax.ShapeDtypeStruct((q_rows + 2 * kv_rows + gate.shape[0], width), BF16),
            jax.ShapeDtypeStruct((q_rows, width), BF16),
            jax.ShapeDtypeStruct((2, ff_rows, width), BF16),
            jax.ShapeDtypeStruct((ff_rows, width), BF16),
        ],
        in_specs=[SMEM_SPEC] + [FAR_SPEC] * 5 + [HBM_SPEC],
        out_specs=[VMEM_SPEC] * 4,
        scratch_shapes=[pltpu.SemaphoreType.DMA((8,))],
        compiler_params=LARGE,
        cost_estimate=pl.CostEstimate(flops=0, bytes_accessed=2**23, transcendentals=0),
        name="slices",
    )(
        sub.reshape(1, 1),
        w_query,
        w_keyval,
        w_outproj,
        w_gateup,
        w_down,
        gate,
    )
    return w_in, wo, wgu.reshape(2 * ff_rows, width), wd


def owned_kernel(spot_ref, *refs):
    ins, outs, sems = refs[:5], refs[-3:-1], refs[-1]
    pairs = []
    for k, out in enumerate(outs):
        spot, at = spot_ref[0, k], 0
        for ref in ins:
            rows = ref.shape[-2] // row_blocks(out, ins)
            span = pl.ds(pl.multiple_of(spot * rows, rows), rows)
            for part in [ref.at[j] for j in range(2)] if len(ref.shape) == 3 else [ref]:
                pairs.append((part.at[span], out.at[pl.ds(at, rows)]))
                at += rows
    run_copies(pairs, sems)


def row_blocks(out, ins):
    total = sum(ref.shape[-2] * (2 if len(ref.shape) == 3 else 1) for ref in ins)
    return total // out.shape[0]


def owned_rows(spots, weights, n, *tokens):
    rows = sum(w.shape[-2] * (2 if w.ndim == 3 else 1) for w in weights) // (4 * n)
    out = jax.ShapeDtypeStruct((rows, weights[0].shape[-1]), BF16)
    return pl.pallas_call(
        owned_kernel,
        out_shape=[out, out],
        in_specs=[SMEM_SPEC] + [FAR_SPEC] * 5 + [HBM_SPEC] * len(tokens),
        out_specs=[VMEM_SPEC] * 2,
        scratch_shapes=[pltpu.SemaphoreType.DMA((14,))],
        compiler_params=LARGE,
        cost_estimate=pl.CostEstimate(flops=0, bytes_accessed=2**22, transcendentals=0),
        name="owned",
    )(spots, *weights, *tokens)


def tie(value, *tokens):
    return pl.pallas_call(
        lambda *refs: None,
        out_shape=jax.ShapeDtypeStruct(value.shape, value.dtype),
        in_specs=[HBM_SPEC] * (1 + len(tokens)),
        out_specs=HBM_SPEC,
        input_output_aliases={0: 0},
        cost_estimate=pl.CostEstimate(flops=0, bytes_accessed=0, transcendentals=0),
        name="tie",
    )(value, *tokens)


def pack_kernel(places, ins, *refs):
    out = refs[-1]
    out[...] = jnp.zeros_like(out)
    for ref, item in zip(refs[:ins], places):
        rows = ref.shape[-2]
        for j, (member, first) in enumerate(item):
            source = ref[j] if len(ref.shape) == 3 else ref[...]
            out[member, first : first + rows] = source.astype(BF16)


def pack(arrays, places, height, *tokens):
    width = arrays[0].shape[-1]
    return pl.pallas_call(
        functools.partial(pack_kernel, places, len(arrays)),
        out_shape=jax.ShapeDtypeStruct((4, height, width), BF16),
        in_specs=[VMEM_SPEC] * len(arrays) + [HBM_SPEC] * len(tokens),
        out_specs=VMEM_SPEC,
        compiler_params=SMALL,
        cost_estimate=pl.CostEstimate(flops=0, bytes_accessed=24 * height * width, transcendentals=0),
        name="pack",
    )(*arrays, *tokens)


def held_kernel(v_ref, *refs):
    refs[-1][...] = v_ref[...]


def held(v, *tokens):
    return pl.pallas_call(
        held_kernel,
        out_shape=jax.ShapeDtypeStruct(v.shape, v.dtype),
        in_specs=[VMEM_SPEC] + [HBM_SPEC] * len(tokens),
        out_specs=VMEM_SPEC,
        compiler_params=SMALL,
        cost_estimate=pl.CostEstimate(flops=0, bytes_accessed=4 * v.size, transcendentals=0),
        name="held",
    )(v, *tokens)


def settle_kernel(places, rates, items, *refs):
    if rates is None:
        count = len(places)
        olds, outs = refs[:count], refs[count:]
    else:
        old_ref, outs = refs[0], refs[1:]
    for a, item in enumerate(places):
        rows = outs[a].shape[-2]
        for j, place in enumerate(item):
            at = (j,) if len(outs[a].shape) == 3 else (slice(None),)
            member, first = place if rates is not None else (place, 0)
            value = items[member, :rows].astype(F32)
            if rates is None:
                outs[a][at] = value
                outs[count + a][at] = 0.5 * olds[a][at] + 0.5 * value
            else:
                old = old_ref[first : first + rows, :].astype(F32)
                outs[a][at] = old - rates[member] * value


def settle(items, olds, shapes, places, rates):
    shapes = [jax.ShapeDtypeStruct(v.shape, F32) for v in shapes]
    shapes = shapes * (2 if rates is None else 1)
    return pl.pallas_call(
        functools.partial(settle_kernel, places, rates),
        out_shape=shapes,
        in_specs=[VMEM_SPEC] * (1 + len(olds)),
        out_specs=[VMEM_SPEC] * len(shapes),
        compiler_params=SMALL,
        cost_estimate=pl.CostEstimate(flops=0, bytes_accessed=12 * items.size, transcendentals=0),
        name="settle",
    )(items, *olds)


TILE = 512
ATTENTION = pltpu.CompilerParams(vmem_limit_bytes=44 * 2**20)


def tile_at(j, size=TILE, offset=0):
    return pl.ds(pl.multiple_of(j * size + offset, size), size)


def shape_of(dtype, *shape):
    return jax.ShapeDtypeStruct(shape, dtype)


def cost(microseconds):
    return pl.CostEstimate(
        flops=int(microseconds * 1.15e9), bytes_accessed=2**20, transcendentals=0
    )


def head_scale(raw):
    return lax.rsqrt(jnp.mean(raw * raw, axis=-1, keepdims=True) + NORM_EPS)


def head_back(grad, raw, cosine, sine, gain):
    grad = grad * cosine - pltpu.roll(grad, grad.shape[1] // 2, 1) * sine
    scale = head_scale(raw)
    unit = raw * scale
    pushed = grad * gain
    back = scale * (pushed - unit * jnp.mean(pushed * unit, axis=-1, keepdims=True))
    return back, jnp.sum(grad * unit, axis=0, keepdims=True)


def project_kernel(heads, n_ref, w_ref, cos_ref, sin_ref, gain_ref, q_ref, kv_ref, lg_ref, raw_ref):
    rows, dim = n_ref.shape[0], cos_ref.shape[1]

    @pl.loop(0, rows // 256)
    def _(t):
        span = tile_at(t, 256)
        out = nt(n_ref[span, :], w_ref[...])
        cosine, sine = cos_ref[span, :], sin_ref[span, :]
        for j in range(heads + 1):
            raw = out[:, j * dim : (j + 1) * dim]
            raw_ref[j, span, :] = raw
            which = slice(0, 1) if j < heads else slice(1, 2)
            unit = raw * head_scale(raw) * gain_ref[which, :]
            turned_rows = unit * cosine + pltpu.roll(unit, dim // 2, 1) * sine
            if j < heads:
                q_ref[j, span, :] = turned_rows.astype(BF16)
            else:
                kv_ref[0, span, :] = turned_rows.astype(BF16)
        kv_ref[1, span, :] = out[:, (heads + 1) * dim : (heads + 2) * dim].astype(BF16)
        lg_ref[span, :] = jax.nn.sigmoid(out[:, (heads + 2) * dim : (heads + 3) * dim])


def project(normed, w_in, cosine, sine, gains):
    rows, dim = cosine.shape
    heads = w_in.shape[0] // dim - 3
    return pl.pallas_call(
        functools.partial(project_kernel, heads),
        out_shape=[
            shape_of(BF16, heads, rows, dim),
            shape_of(BF16, 2, rows, dim),
            shape_of(F32, rows, dim),
            shape_of(F32, heads + 1, rows, dim),
        ],
        in_specs=[VMEM_SPEC] * 5,
        out_specs=[VMEM_SPEC] * 4,
        compiler_params=ATTENTION,
        cost_estimate=cost(6),
        name="project",
    )(normed, w_in, cosine, sine, gains)


def widened(values):
    return jnp.concatenate([values, jnp.ones_like(values)], axis=1)


def attend_kernel(scale, q_ref, lg_ref, qp_ref, kp_ref, *refs):
    pieces, (att_ref, tot_ref, gated_ref) = refs[:-3], refs[-3:]
    heads, rows, dim = q_ref.shape
    for h in range(heads):

        @pl.loop(0, rows // TILE)
        def _(i):
            span = tile_at(i)
            query, place = q_ref[h, span, :], qp_ref[span, :]
            total = jnp.zeros((TILE, 2 * dim), F32)
            for number, kv_ref in enumerate(pieces):
                offset = number * kv_ref.shape[1]

                def step(j, acc, kv_ref=kv_ref, offset=offset):
                    scores = nt(query, kv_ref[0, tile_at(j), :])
                    seen = kp_ref[:, tile_at(j, offset=offset)] <= place
                    weights = jnp.where(seen, jnp.exp2(scores * scale), 0.0)
                    return acc + nn(weights.astype(BF16), widened(kv_ref[1, tile_at(j), :]))

                total = lax.fori_loop(0, kv_ref.shape[1] // TILE, step, total)
            weight = total[:, dim : dim + 1]
            attended = total[:, :dim] / weight
            att_ref[h, span, :] = attended
            tot_ref[h, span, :] = weight
            gated_ref[span, h * dim : (h + 1) * dim] = (
                attended * lg_ref[span, h : h + 1]
            ).astype(BF16)


def attend(query, sigmoids, pieces, q_place, k_place, scale, *tokens):
    heads, rows, dim = query.shape
    count = len(pieces)
    kernel = functools.partial(attend_kernel, scale * math.log2(math.e))

    def without_tokens(*refs):
        kernel(*refs[: 4 + count], *refs[4 + count + len(tokens) :])

    return pl.pallas_call(
        without_tokens,
        out_shape=[
            shape_of(F32, heads, rows, dim),
            shape_of(F32, heads, rows, 1),
            shape_of(BF16, rows, heads * dim),
        ],
        in_specs=[VMEM_SPEC] * (4 + count) + [HBM_SPEC] * len(tokens),
        out_specs=[VMEM_SPEC] * 3,
        compiler_params=ATTENTION,
        cost_estimate=cost(12),
        name="attend",
    )(query, sigmoids, q_place[:, None], k_place[None, :], *pieces, *tokens)


def before_kernel(b_ref, w_ref, att_ref, tot_ref, lg_ref, bw_ref, dl_ref):
    heads, rows, dim = att_ref.shape
    lanes = lax.broadcasted_iota(jnp.int32, (256, dim), 1)

    @pl.loop(0, rows // 256)
    def _(t):
        span = tile_at(t, 256)
        grad = nt(b_ref[span, :], w_ref[...])
        logits = jnp.zeros((256, dim), F32)
        for h in range(heads):
            part = grad[:, h * dim : (h + 1) * dim]
            sig = lg_ref[span, h : h + 1]
            total = tot_ref[h, span, :]
            along = jnp.sum(part * att_ref[h, span, :], axis=-1, keepdims=True)
            logits = jnp.where(lanes == h, sig * (1.0 - sig) * along, logits)
            bw_ref[h, span, :dim] = (part * (sig / total)).astype(BF16)
            corr = -sig * along / total
            high = corr.astype(BF16).astype(F32)
            extra = jnp.where(lanes == 0, high, jnp.where(lanes == 1, corr - high, 0.0))
            bw_ref[h, span, dim:] = extra.astype(BF16)
        dl_ref[span, :] = logits.astype(BF16)


def before_attention(dbranch, wo, attended, total, sigmoids):
    heads, rows, dim = attended.shape
    return pl.pallas_call(
        before_kernel,
        out_shape=[shape_of(BF16, heads, rows, 2 * dim), shape_of(BF16, rows, dim)],
        in_specs=[VMEM_SPEC] * 5,
        out_specs=[VMEM_SPEC] * 2,
        compiler_params=ATTENTION,
        cost_estimate=cost(5),
        name="before",
    )(dbranch, wo, attended, total, sigmoids)


def attend_back_kernel(
    scale, count, q_ref, bw_ref, raw_ref, cos_ref, sin_ref, gain_ref, qp_ref, kp_ref, *refs
):
    pieces = refs[:count]
    dq_ref, terms_ref = refs[count : count + 2]
    outs, sums = refs[count + 2 : 2 * count + 2], refs[2 * count + 2 :]
    heads, rows, dim = q_ref.shape
    grow = scale * math.log2(math.e)
    for ref in sums:
        ref[...] = jnp.zeros_like(ref)
    terms_ref[...] = jnp.zeros_like(terms_ref)
    for h in range(heads):

        @pl.loop(0, rows // TILE)
        def _(i):
            span = tile_at(i)
            query, back, place = q_ref[h, span, :], bw_ref[h, span, :], qp_ref[:, span]
            total = jnp.zeros((TILE, dim), F32)
            for number, (kv_ref, sum_ref) in enumerate(zip(pieces, sums)):
                offset = number * kv_ref.shape[1]

                def step(j, acc, kv_ref=kv_ref, sum_ref=sum_ref, offset=offset):
                    keys = tile_at(j)
                    key = kv_ref[0, keys, :]
                    seen = kp_ref[tile_at(j, offset=offset), :] <= place
                    weights = jnp.where(seen, jnp.exp2(nt(key, query) * grow), 0.0)
                    push = nt(widened(kv_ref[1, keys, :]), back)
                    dscore = (weights * push * scale).astype(BF16)
                    sum_ref[1, keys, :] += nn(weights.astype(BF16), back[:, :dim])
                    sum_ref[0, keys, :] += nn(dscore, query)
                    return acc + tn(dscore, key)

                total = lax.fori_loop(0, kv_ref.shape[1] // TILE, step, total)
            grad, terms = head_back(
                total, raw_ref[h, span, :], cos_ref[span, :], sin_ref[span, :], gain_ref[0:1, :]
            )
            dq_ref[span, h * dim : (h + 1) * dim] = grad.astype(BF16)
            terms_ref[...] += terms

    for out, ref in zip(outs, sums):
        out[...] = ref[...].astype(out.dtype)


def attend_back(query, back, raw, cosine, sine, gains, pieces, q_place, k_place, scale):
    heads, rows, dim = query.shape
    count = len(pieces)
    return pl.pallas_call(
        functools.partial(attend_back_kernel, scale, count),
        out_shape=[shape_of(BF16, rows, heads * dim), shape_of(F32, 1, dim)]
        + [shape_of(BF16 if k else F32, *piece.shape) for k, piece in enumerate(pieces)],
        in_specs=[VMEM_SPEC] * (8 + count),
        out_specs=[VMEM_SPEC] * (2 + count),
        scratch_shapes=[pltpu.VMEM(piece.shape, F32) for piece in pieces],
        compiler_params=ATTENTION,
        cost_estimate=cost(18),
        name="attend_back",
    )(
        query, back, raw, cosine, sine, gains, q_place[None, :], k_place[:, None], *pieces
    )


def keys_kernel(own_ref, far_ref, raw_ref, cos_ref, sin_ref, gain_ref, dl_ref, out_ref, terms_ref):
    rows, dim = cos_ref.shape
    terms_ref[...] = jnp.zeros_like(terms_ref)

    @pl.loop(0, rows // 256)
    def _(t):
        span = tile_at(t, 256)
        both = [own_ref[k, span, :] + far_ref[k, span, :].astype(F32) for k in range(2)]
        grad, terms = head_back(
            both[0], raw_ref[raw_ref.shape[0] - 1, span, :], cos_ref[span, :], sin_ref[span, :], gain_ref[1:2, :]
        )
        terms_ref[...] += terms
        out_ref[span, :dim] = grad.astype(BF16)
        out_ref[span, dim : 2 * dim] = both[1].astype(BF16)
        out_ref[span, 2 * dim :] = dl_ref[span, :]


def keys_back(own, far, raw, cosine, sine, gains, dlogit):
    rows, dim = cosine.shape
    return pl.pallas_call(
        keys_kernel,
        out_shape=[shape_of(BF16, rows, 3 * dim), shape_of(F32, 1, dim)],
        in_specs=[VMEM_SPEC] * 7,
        out_specs=[VMEM_SPEC] * 2,
        compiler_params=ATTENTION,
        cost_estimate=cost(3),
        name="keys",
    )(own, far, raw, cosine, sine, gains, dlogit)


def rms_scale(v):
    return lax.rsqrt(jnp.mean(v * v, axis=-1, keepdims=True) + NORM_EPS)


def norm_back(grad, scaled, rscale, gains):
    pushed = grad * gains
    return rscale * (pushed - scaled * jnp.mean(pushed * scaled, axis=-1, keepdims=True))


def mirror(ref, tile):
    for j in range(ref.shape[0] // tile):
        for i in range(j):
            block = ref[i * tile : (i + 1) * tile, j * tile : (j + 1) * tile].astype(F32)
            ref[j * tile : (j + 1) * tile, i * tile : (i + 1) * tile] = block.T.astype(BF16)


def schulz_kernel(count, start_ref, *refs):
    pieces = refs[:count]
    o_ref, x_ref, x_own, e_gram, e_poly, e_half, gram, poly, half, sems = refs[-10:]
    piece = pieces[0].shape[0]
    copies = [
        pltpu.make_async_copy(ref, x_ref.at[pl.ds(k * piece, piece)], sems.at[k])
        for k, ref in enumerate(pieces)
    ]
    for copy in copies:
        copy.start()
    for copy in copies:
        copy.wait()
    chunk = min(1024, x_ref.shape[0])
    width = x_ref.shape[1]
    own = o_ref.shape[0]
    tile = 256
    blocks = [(slice(0, (j + 1) * tile), slice(j * tile, (j + 1) * tile)) for j in range(width // tile)]
    diag = (
        lax.broadcasted_iota(jnp.int32, (tile, tile), 0)
        == lax.broadcasted_iota(jnp.int32, (tile, tile), 1)
    ).astype(F32)

    def trace(ref):
        total = jnp.zeros((tile, tile), F32)
        for _, cols in blocks:
            total = total + ref[cols, cols] * diag
        return jnp.sum(jnp.sum(total, axis=1, keepdims=True), axis=0, keepdims=True)

    def settle_gram(scale, centre):
        for rows, cols in blocks:
            part = e_gram[rows, cols]
            e_gram[rows, cols] = part if scale is None else part * scale
            e_gram[cols, cols] -= centre * diag
            gram[rows, cols] = e_gram[rows, cols].astype(BF16)
        mirror(gram, tile)

    def make_poly(d):
        p = NS_A + NS_B * d + NS_C * d * d
        for rows, cols in blocks:
            part = (NS_B + 2.0 * NS_C * d) * e_gram[rows, cols] + NS_C * nn(
                gram[rows, :], gram[:, cols]
            )
            e_poly[rows, cols] = part
            poly[rows, cols] = part.astype(BF16)
        mirror(poly, tile)
        return p

    def advance(d, p):
        for rows, cols in blocks:
            part = d * e_poly[rows, cols] + p * e_gram[rows, cols] + nn(gram[rows, :], poly[:, cols])
            e_half[rows, cols] = part
            half[rows, cols] = part.astype(BF16)
        mirror(half, tile)
        q = d * p
        for rows, cols in blocks:
            e_gram[rows, cols] = (
                q * e_poly[rows, cols] + p * e_half[rows, cols] + nn(half[rows, :], poly[:, cols])
            )
        centre = trace(e_gram) * (1.0 / width)
        settle_gram(None, centre)
        return q * p + centre

    def apply(p):
        now = x_own[...]
        return p * now + nn(now.astype(BF16), poly[...])

    for rows, cols in blocks:
        e_gram[rows, cols] = lax.fori_loop(
            0,
            x_ref.shape[0] // chunk,
            lambda r, acc: acc
            + tn(
                x_ref[pl.ds(pl.multiple_of(r * chunk, chunk), chunk), rows],
                x_ref[pl.ds(pl.multiple_of(r * chunk, chunk), chunk), cols],
            ),
            jnp.zeros((rows.stop, tile), F32),
        )
    square = trace(e_gram)
    inv = 1.0 / (jnp.sqrt(square) + 1e-07)
    first = square * inv * inv * (1.0 / width)
    settle_gram(inv * inv, first)
    x_own[...] = x_ref[pl.ds(pl.multiple_of(start_ref[0, 0], own), own), :].astype(F32) * inv

    def sweep(_, d):
        p = make_poly(d)
        x_own[...] = apply(p)
        return advance(d, p)

    d = lax.fori_loop(0, NS_STEPS - 1, sweep, first)
    o_ref[...] = apply(make_poly(d)).astype(BF16)


def orthogonal(pieces, firsts, own, *tokens):
    count = len(pieces)
    rows, width = count * pieces[0].shape[0], pieces[0].shape[1]
    wide = pltpu.VMEM((width, width), F32)
    low = pltpu.VMEM((width, width), BF16)
    return pl.pallas_call(
        functools.partial(schulz_kernel, count),
        out_shape=jax.ShapeDtypeStruct((own, width), BF16),
        in_specs=[SMEM_SPEC] + [HBM_SPEC] * (count + len(tokens)),
        out_specs=VMEM_SPEC,
        scratch_shapes=[
            pltpu.VMEM((rows, width), BF16),
            pltpu.VMEM((own, width), F32),
            wide,
            wide,
            wide,
            low,
            low,
            low,
            pltpu.SemaphoreType.DMA((count,)),
        ],
        compiler_params=pltpu.CompilerParams(vmem_limit_bytes=48 * 2**20),
        cost_estimate=pl.CostEstimate(
            flops=44 * 2**30, bytes_accessed=4 * rows * width, transcendentals=0
        ),
        name="schulz",
    )(firsts, *pieces, *tokens)


def on_device(
    n,
    tokens,
    cotangent,
    pair_order,
    norm_gains,
    head_gains,
    gate_head,
    w_query,
    w_keyval,
    w_outproj,
    w_gateup,
    w_down,
    mom_norm,
    mom_head,
    mom_gate_head,
    mom_query,
    mom_keyval,
    mom_outproj,
    mom_gateup,
    mom_down,
):
    quarter = n // 4
    my_h, my_m, my_i = lax.axis_index("h"), lax.axis_index("m"), lax.axis_index("i")
    my_b, my_c, my_x = lax.axis_index("b"), lax.axis_index("c"), lax.axis_index("x")
    me = lax.axis_index(ALL)
    everywhere = ("h", "m", "i")
    sub = my_c * 2 + my_b
    my_plane = my_h * 2 + my_m
    tok_dev, width = tokens.shape[1], tokens.shape[2]
    head_dim = head_gains.shape[1]
    scale = 1.0 / math.sqrt(head_dim)
    piece = tok_dev // 2
    group_rows = 8 * tok_dev

    rows_tok = swap_halves(tokens[0], my_h, my_x)
    xf = rows_tok.astype(F32)
    r1 = rms_scale(xf)
    y1 = xf * r1
    normed_rows = (y1 * norm_gains[0]).astype(BF16)
    q_rows = w_query.shape[0] // 4
    kv_rows = w_keyval.shape[1] // 4
    heads_here = q_rows // head_dim
    wgate = lax.dynamic_slice_in_dim(gate_head, (my_x * 4 + sub) * heads_here, heads_here, 0)
    gate_pad = 128 - heads_here
    small_block = w_keyval.shape[1] // (4 * n)
    out_block = w_outproj.shape[0] // (4 * n)
    ff_block = w_gateup.shape[1] // (4 * n)
    ff_rows = n * ff_block
    w_in, wo, wgu, wd = weight_slices(
        sub,
        w_query,
        w_keyval,
        w_outproj,
        w_gateup,
        w_down,
        jnp.pad(wgate, ((0, gate_pad), (0, 0))),
    )


    order_ids = jnp.arange(pair_order.shape[0], dtype=jnp.int32)

    def group_place(r_index):
        flips = jnp.arange(8, dtype=jnp.int32)
        dev_x = my_x ^ (flips & 1)
        dev_b = my_b ^ ((flips >> 1) & 1)
        dev_c = my_c ^ (flips >> 2)
        ctx_ids = ((dev_x * (n // 2) + r_index) * 2 + dev_b) * 2 + dev_c
        owner = jnp.sum(
            jnp.where(ctx_ids[:, None] == order_ids[None, :], pair_order[None, :], 0), axis=1
        )
        blocks = jnp.stack([owner, 2 * pair_order.shape[0] - 1 - owner], axis=1)
        spots = blocks[:, :, None] * piece + jnp.arange(piece, dtype=jnp.int32)
        return spots.reshape(group_rows)

    my_r = my_m * quarter + my_i
    place = group_place(my_r)
    if n == 4:
        key_place = jnp.concatenate([place, group_place(my_r ^ 1)])
    else:
        key_place = jnp.concatenate([group_place(r) for r in range(n // 2)])

    def key_pieces(kv):
        if n == 4:
            return [kv, flip(kv, "m")]
        return [lax.all_gather(kv, ("m", "i"), axis=1, tiled=True)]

    def key_sums(parts):
        if n == 4:
            return parts[0], flip(parts[1], "m")
        mine = lax.psum_scatter(parts[0], ("m", "i"), scatter_dimension=1, tiled=True)
        return mine, jnp.zeros(mine.shape, BF16)

    half = head_dim // 2
    inverse = ROPE_BASE ** (-(2.0 * jnp.arange(half, dtype=F32)) / head_dim)
    angles = place.astype(F32)[:, None] * inverse[None, :]
    cosine, sine = jnp.cos(angles), jnp.sin(angles)
    cosine = jnp.concatenate([cosine, cosine], axis=1)
    sine = jnp.concatenate([-sine, sine], axis=1)
    normed_rows = tie(normed_rows, w_in, cosine, sine, key_place)
    normed = gather_group(normed_rows)
    query_rows, kv_rows_here, sigmoids, raw = project(normed, w_in, cosine, sine, head_gains)
    rows_cot = swap_halves(held(cotangent[0], w_in, cosine), my_h, my_x)
    kv_all = key_pieces(kv_rows_here)
    cot_near = gather_near(tie(rows_cot, query_rows))
    attended, total, gated = attend(
        query_rows, sigmoids, kv_all, place, key_place, scale, rows_cot
    )
    gated = tie(gated, *cot_near)

    first_moms = (mom_gateup, mom_down)
    first_places = ((GATE, UP), (DOWN,))
    second_moms = (mom_query, mom_keyval, mom_outproj)
    second_places = ((QUERY,), (KEY, VALUE), (OUT,))
    old_items = pack(
        first_moms + second_moms,
        [[(member, 0) for member in place] for place in first_places]
        + [[(member, ff_block) for member in place] for place in second_places],
        ff_block + out_block,
        query_rows,
    )
    if quarter > 1:
        old_items = lax.ppermute(old_items, ("i", "b"), [(d, p) for p, d in fold_pairs(quarter)])
    old_items = trade(old_items, ("h", "m"))

    middle = xf + sum_group(nn(gated, wo))
    grad_all = gather_far(cot_near)
    r2 = rms_scale(middle)
    y2 = middle * r2
    hidden_in = gather_group((y2 * norm_gains[1]).astype(BF16))
    gate_up = nt(hidden_in, wgu)
    gate_part, up_part = gate_up[:, :ff_rows], gate_up[:, ff_rows:]
    sg = jax.nn.sigmoid(gate_part)
    silu = gate_part * sg
    hidden = (silu * up_part).astype(BF16)

    dhidden = nt(grad_all, wd)
    dgu = jnp.concatenate(
        [
            (dhidden * up_part * sg * (1.0 + gate_part * (1.0 - sg))).astype(BF16),
            (dhidden * silu).astype(BF16),
        ],
        axis=1,
    )
    dgu = tie(dgu, old_items)
    grad_gu = tn(dgu, hidden_in).astype(BF16)
    grad_d = tn(hidden, grad_all).astype(BF16)
    ff_grad = lax.psum_scatter(
        jnp.concatenate([grad_d, jnp.zeros_like(grad_d), grad_gu], axis=0),
        ("h", "m", "i"),
        scatter_dimension=0,
        tiled=True,
    )
    dhn = sum_group(nn(dgu, wgu))
    gout = rows_cot.astype(F32)
    norm_terms_mid = jnp.sum(dhn * y2, axis=0)
    dmiddle = gout + norm_back(dhn, y2, r2, norm_gains[1])
    out_sum = sum_core(nn(hidden, wd))
    dbranch = gather_group(tie(dmiddle.astype(BF16), out_sum))

    back_w, dlogit = before_attention(dbranch, wo, attended, total, sigmoids)

    def over_i(v):
        return lax.psum_scatter(v, "i", scatter_dimension=0, tiled=True) if quarter > 1 else v

    def blend(old, grad):
        return (0.5 * old.astype(F32) + 0.5 * grad.astype(F32)).astype(BF16)

    def padded(v, rows, height):
        blocks = v.reshape(4, rows, width)
        return jnp.pad(blocks, ((0, 0), (0, height - rows), (0, 0)))

    everyone = ("i", "b", "c", "x")
    mine_at = lax.axis_index(everyone)

    grad_o = over_i(tn(gated, dbranch).astype(BF16))
    grad_o = grad_o.astype(F32) + lax.ppermute(grad_o, ("h", "m"), [(0, 1), (3, 2)]).astype(F32)
    first_grad = ff_grad.reshape(4, ff_block, width)
    out_sum = tie(out_sum, back_w)

    dq, query_terms, *kv_sums = attend_back(
        query_rows, back_w, raw, cosine, sine, head_gains, kv_all, place, key_place, scale
    )
    out_rows = middle + sum_near(out_sum)
    first_mid = turned(trade(tie(first_grad, dq), ("c", "x")))
    kv_sums[0] = tie(kv_sums[0], out_rows)
    first_old, second_old = old_items[:, :ff_block], old_items[:, ff_block:]
    first_block = blend(first_old, first_mid).reshape(4 * ff_block, width)
    kv_own, kv_far = key_sums(kv_sums)
    dkv, key_terms = keys_back(kv_own, kv_far, raw, cosine, sine, head_gains, dlogit)
    first_start = lax.all_gather(tie(first_block, dkv), everyone, axis=0, tiled=True)
    head_terms = jnp.concatenate([query_terms, key_terms], axis=0)
    grad_q, grad_kv = tn(dq, normed), tn(dkv, normed)
    query_part = grad_q.reshape(n, 2, small_block, width)
    second_part = jnp.concatenate(
        [
            jnp.transpose(query_part, (1, 0, 2, 3)).reshape(q_rows, width),
            grad_kv[: 2 * kv_rows],
        ],
        axis=0,
    ).astype(BF16)
    dn_core = sum_core(nn(dq, w_in[:q_rows]) + nn(dkv, w_in[q_rows:]))
    dnormed = sum_near(dn_core)
    norm_terms_in = jnp.sum(dnormed * y1, axis=0)
    grad_rows = dmiddle + norm_back(dnormed, y1, r1, norm_gains[0])
    if quarter > 1:
        second_part = second_part.reshape(4, quarter, -1, width)
        second_part = lax.psum_scatter(second_part, "i", scatter_dimension=1, tiled=True)
    second_part = second_part.reshape(4, 4 * small_block, width)
    chunks = [
        lax.dynamic_index_in_dim(second_part, my_plane ^ k, 0, keepdims=False) for k in range(4)
    ]
    mine = chunks[0].astype(F32)
    for k, axes in ((1, ("m",)), (2, ("h",)), (3, ("h", "m"))):
        mine = mine + flip(chunks[k], *axes).astype(F32)
    mine = tie(mine.astype(BF16), dn_core)
    mine_sum = mine
    grad_o = tie(grad_o, mine_sum)
    grad_o = grad_o + lax.ppermute(grad_o.astype(BF16), ("h", "m"), [(2, 1)]).astype(F32)
    pair = flip(mine, "m")
    mine, pair = (v.reshape(4, small_block, width) for v in (mine, pair))
    second_grad = jnp.concatenate(
        [mine, jnp.where(my_plane == QUERY, pair, jnp.zeros_like(pair))], axis=1
    )
    second_grad = jnp.where(
        my_plane == OUT, grad_o.astype(BF16).reshape(4, out_block, width), second_grad
    )
    second_mid = turned(trade(second_grad, ("c", "x")))
    second_block = blend(second_old, second_mid).reshape(4 * out_block, width)
    small_z = (
        jnp.concatenate(
            [
                lax.dynamic_update_slice_in_dim(
                    jnp.zeros((gate_head.shape[0], width), F32),
                    grad_kv[2 * kv_rows : 2 * kv_rows + heads_here],
                    (my_x * 4 + sub) * heads_here,
                    0,
                ),
                norm_terms_in[None],
                norm_terms_mid[None],
                jnp.pad(head_terms.reshape(1, 2 * head_dim), ((0, 0), (0, width - 2 * head_dim))),
            ],
            axis=0,
        )
    )
    small = sum_flips(small_z, (("m",), ("h",), ("h", "m")))
    if quarter > 1:
        small = lax.psum(small, "i")
    small = sum_flips(small, NEAR)
    second_block = tie(second_block, small)
    second_start = lax.all_gather(second_block, everyone, axis=0, tiled=True)
    spot = me % (4 * n)
    mine_now, other_now = owned_rows(
        jnp.stack([spot, spot ^ 1]).reshape(1, 2),
        (w_query, w_keyval, w_outproj, w_gateup, w_down),
        n,
        second_block,
    )
    first_g = trade(tie(first_mid, second_block), ("h", "m"))
    if quarter > 1:
        first_g = lax.ppermute(first_g, ("i", "b"), fold_pairs(quarter))
    first_ortho = orthogonal(
        [first_start], (mine_at * (4 * ff_block)).reshape(1, 1), 4 * ff_block, other_now
    )
    second_ortho = orthogonal([second_start], (mine_at * (4 * out_block)).reshape(1, 1), 4 * out_block, first_ortho)
    sent = lax.ppermute(tie(grad_rows.astype(BF16), first_ortho), ("h", "x"), [(1, 2), (2, 1)])
    grad_input = jnp.where(my_h == my_x, grad_rows, sent.astype(F32))
    first_g = tie(first_g, first_ortho)
    returned = jnp.concatenate(
        [first_ortho.reshape(4, ff_block, width), tie(second_mid, first_ortho)], axis=1
    )
    returned = trade(tie(returned, first_g), ("h", "m"))
    if quarter > 1:
        returned = lax.ppermute(returned, ("i", "b"), fold_pairs(quarter))
    first_x, second_g = returned[:, :ff_block], returned[:, ff_block:]
    old_rows = jnp.where(my_x == my_h, mine_now, flip(tie(other_now, first_ortho), "x"))
    output = swap_halves(tie(out_rows.astype(BF16), first_ortho), my_h, my_x)
    second_ortho = tie(second_ortho, returned, old_rows)
    second_x = trade(second_ortho.reshape(4, out_block, width), ("h", "m"))
    if quarter > 1:
        second_x = lax.ppermute(second_x, ("i", "b"), fold_pairs(quarter))


    head_count = gate_head.shape[0]
    small = sum_flips(tie(small, second_ortho), (("c",),))
    grad_gate = small[:head_count]
    grad_norm = small[head_count : head_count + 2]
    grad_head = small[head_count + 2, : 2 * head_dim].reshape(2, head_dim)
    new_mom_norm = 0.5 * mom_norm + 0.5 * grad_norm
    new_mom_head = 0.5 * mom_head + 0.5 * grad_head
    new_mom_gate = 0.5 * mom_gate_head + 0.5 * grad_gate
    new_norm = norm_gains - VECTOR_RATE * new_mom_norm
    new_head = head_gains - VECTOR_RATE * new_mom_head
    new_gate = gate_head.astype(F32) - VECTOR_RATE * new_mom_gate

    seq_len = tok_dev * n * 4
    out_boost = math.sqrt(width / max(1, 16384 // seq_len))
    rate = lambda rows: MATRIX_RATE * math.sqrt(rows * 8 * n)
    first_rates = {DOWN: rate(ff_block), GATE: rate(ff_block), UP: rate(ff_block)}
    second_rates = {
        QUERY: rate(out_block),
        OUT: out_boost * rate(out_block),
        KEY: rate(small_block),
        VALUE: rate(small_block),
    }
    q_at, k_at, v_at = 0, out_block, out_block + small_block
    o_at = v_at + small_block
    gate_at, up_at, down_at = (o_at + out_block + k * ff_block for k in range(3))
    g_gateup, g_down, m_gateup, m_down = settle(
        first_g, first_moms, first_moms, first_places, None
    )
    g_query, g_keyval, g_outproj, m_query, m_keyval, m_outproj = settle(
        second_g, second_moms, second_moms, second_places, None
    )
    n_gateup, n_down = settle(
        first_x,
        [old_rows],
        first_moms,
        (((GATE, gate_at), (UP, up_at)), ((DOWN, down_at),)),
        first_rates,
    )
    n_query, n_keyval, n_outproj = settle(
        second_x,
        [old_rows],
        second_moms,
        (((QUERY, q_at),), ((KEY, k_at), (VALUE, v_at)), ((OUT, o_at),)),
        second_rates,
    )

    return (
        output[None],
        grad_input[None],
        grad_norm,
        grad_head,
        grad_gate,
        g_query,
        g_keyval,
        g_outproj,
        g_gateup,
        g_down,
        new_mom_norm,
        new_mom_head,
        new_mom_gate,
        m_query,
        m_keyval,
        m_outproj,
        m_gateup,
        m_down,
        new_norm,
        new_head,
        new_gate,
        n_query,
        n_keyval,
        n_outproj,
        n_gateup,
        n_down,
    )


def solution(mesh):
    count = mesh.devices.size
    n = count // 8
    sizes = {"h": 2, "m": 2, "i": n // 4, "b": 2, "c": 2, "x": 2}
    fine = Mesh(mesh.devices.reshape(tuple(sizes[axis] for axis in ALL)), ALL)
    rows3 = P("x", CTX, None)
    own2 = P(ALL, None)
    own3 = P(None, ALL, None)
    half2 = P("x", None)
    half3 = P(None, "x", None)
    owners = (own2, own3, own2, own3, own2)
    return jax.shard_map(
        functools.partial(on_device, n),
        mesh=fine,
        in_specs=(rows3, rows3, P(), P(), P(), P(), half2, half3, half2, half3, half2)
        + (P(), P(), P())
        + owners,
        out_specs=(rows3, rows3, P(), P(), P())
        + owners
        + (P(), P(), P())
        + owners
        + (P(), P(), P())
        + owners,
        check_vma=False,
    )
```
